32 devices in a mesh: replica: 8 (over z, x), group: 4 (over y, core).
Axes of the slice: x: 2, y: 2, z: 4, core: 2. Of those that a mesh axis runs over, the one named last changes fastest.
Arguments:
- inputs: bfloat16 [8192, 576], P(('replica', 'group')), may hold values from -6 to 6
- seg_ids: int32 [8192], P(('replica', 'group')), may hold values from 0 to 4, as said below
- seq_starts: int32 [6], replicated, may hold values from 0 to 8192, as said below
- gain_one: bfloat16 [576], P('group'), may hold values from 0.099609375 to 1.8984375
- query_w: bfloat16 [576, 576], P('group'), may hold values from -0.25 to 0.25
- key_w: bfloat16 [576, 192], P('group'), may hold values from -0.25 to 0.25
- value_weight: bfloat16 [576, 192], P('group'), may hold values from -0.25 to 0.25
- out_w: bfloat16 [576, 576], P('group'), may hold values from -2 to 2
- gain_two: bfloat16 [576], P('group'), may hold values from 0.099609375 to 1.8984375
- gate_w: bfloat16 [576, 1536], P('group'), may hold values from -0.25 to 0.25
- up_w: bfloat16 [576, 1536], P('group'), may hold values from -0.25 to 0.25
- down_w: bfloat16 [1536, 576], P('group'), may hold values from -0.15625 to 0.15625
- out_grad: bfloat16 [8192, 576], P(('replica', 'group')), may hold values from -6 to 6
Outputs:
- outputs: float32 [8192, 576], P(('replica', 'group'))
- grad_inputs: float32 [8192, 576], P(('replica', 'group'))
- grad_gain_one: float32 [576], P('group')
- grad_query_w: float32 [576, 576], P('group')
- grad_key_w: float32 [576, 192], P('group')
- grad_value_w: float32 [576, 192], P('group')
- grad_out_w: float32 [576, 576], P('group')
- grad_gain_two: float32 [576], P('group')
- grad_gate_w: float32 [576, 1536], P('group')
- grad_up_w: float32 [576, 1536], P('group')
- grad_down_w: float32 [1536, 576], P('group')
The draws below stay inside these ranges and needn't reach their ends.
Inputs may be any that keep to these rules, and one draw needn't show every extreme that they name: seq_starts[0] is 0, seq_starts[1] lies between 1 and 2047, each later entry up to index 4 is 2048 more than the one before, and the last entry, at index 5, is 8192. seg_ids[i] is the number of entries of seq_starts after the first that are at most i; every sequence but the first and the last holds 2048 tokens.
All inputs are finite; a program needn't handle non-finite values.
Results may differ from the reference program's by a relative error of at most 0.017.
Values may be sent and summed in bfloat16 or wider, within the bound.
A program may use at most 128 MiB of HBM per device.

```python
import math
import jax
import jax.numpy as jnp
from jax import lax

D = 576
FF = 1536
QUERY_HEADS = 9
KEY_VALUE_HEADS = 3
HEAD_DIM = 64
TOK_DEV = 256
SEQUENCE_LENGTH = 2048
QD = 576
KVD = 192
TOKEN_COUNT = 8192
NSEG = 5


def pack_offset(key):
    first_key, second_key = jax.random.split(key)
    whole_blocks = jax.random.randint(first_key, (), 0, SEQUENCE_LENGTH // TOK_DEV)
    extra_rows = jax.random.randint(second_key, (), 1, TOK_DEV)
    return (whole_blocks * TOK_DEV + extra_rows).astype(jnp.int32)


def draw_seg_ids(key, part):
    offset = pack_offset(key)
    token_index = jnp.arange(TOKEN_COUNT, dtype=jnp.int32)
    later = jnp.maximum(token_index - offset, 0) // SEQUENCE_LENGTH
    return jnp.where(token_index < offset, 0, 1 + later).astype(jnp.int32)


def draw_seq_starts(key, part):
    offset = pack_offset(key)
    order = jnp.arange(NSEG + 1, dtype=jnp.int32)
    starts = jnp.where(order == 0, 0, offset + (order - 1) * SEQUENCE_LENGTH)
    return jnp.where(order == NSEG, TOKEN_COUNT, starts).astype(jnp.int32)


def block_levels(rng, dims, cuts, low, top_value):
    level = 1.0
    for dim, blocks in cuts:
        draws = jax.random.uniform(jax.random.fold_in(jax.random.fold_in(rng, 6), dim), (blocks,), jnp.float32, low / len(cuts), top_value / len(cuts))
        level = level * jnp.repeat(jnp.exp(draws), dims[dim] // blocks).reshape((-1,) + (1,) * (len(dims) - 1 - dim))
    return level


def noise(stream_key, extent, scale, reach, pieces=(), held_as=jnp.bfloat16):
    gain = block_levels(stream_key, extent, pieces, -0.22, 0.18) if pieces else 1.0
    result = jax.random.normal(stream_key, extent, jnp.float32) * scale * gain
    return jnp.minimum(jnp.maximum(result, -reach), reach).astype(held_as)


def setup_inputs(seed: int = 0) -> dict:
    key_list = jax.random.split(jax.random.key(seed), 14)
    return {
        "inputs": noise(key_list[0], (TOKEN_COUNT, D), 1.0, 6.0, ((0, 32),)),
        "seg_ids": draw_seg_ids(jax.random.fold_in(key_list[13], 71), 0),
        "seq_starts": draw_seq_starts(jax.random.fold_in(key_list[13], 71), 0),
        "gain_one": jnp.clip(1.0 + 0.18 * jax.random.normal(key_list[3], (D,), jnp.float32), 0.099609375, 1.8984375).astype(jnp.bfloat16),
        "query_w": noise(key_list[4], (D, QD), D ** -0.5, 0.25, ((0, 4),)),
        "key_w": noise(key_list[5], (D, KVD), D ** -0.5, 0.25, ((0, 4),)),
        "value_weight": noise(key_list[6], (D, KVD), D ** -0.5, 0.25, ((0, 4),)),
        "out_w": noise(key_list[7], (QD, D), (max(QD // 64, 1)) ** -0.5, 2.0, ((0, 4),)),
        "gain_two": jnp.clip(1.0 + 0.18 * jax.random.normal(key_list[8], (D,), jnp.float32), 0.099609375, 1.8984375).astype(jnp.bfloat16),
        "gate_w": noise(key_list[9], (D, FF), D ** -0.5, 0.25, ((0, 4),)),
        "up_w": noise(key_list[10], (D, FF), D ** -0.5, 0.25, ((0, 4),)),
        "down_w": noise(key_list[11], (FF, D), FF ** -0.5, 0.15625, ((0, 4),)),
        "out_grad": noise(key_list[12], (TOKEN_COUNT, D), 1.0, 6.0, ((0, 32),)),
    }


epsilon = 1e-05
rope_base = 100000.0
masked_score = -1e+30
highest = lax.Precision.HIGHEST

@jax.custom_vjp
def reduced_precision(v):
    return lax.optimization_barrier(v.astype(jnp.bfloat16)).astype(jnp.float32)

@jax.custom_vjp
def reduced_precision_back(v):
    return v

def low_keep(v):
    return (reduced_precision(v), None)

def low_pass(kept, grad):
    return (grad,)

def back_keep(v):
    return (v, None)

def back_low(kept, grad):
    return (reduced_precision(grad),)
reduced_precision.defvjp(low_keep, low_pass)
reduced_precision_back.defvjp(back_keep, back_low)

def matrix_multiply(former, latter):
    return jnp.dot(former, latter, precision=highest, preferred_element_type=jnp.float32)

def rms_scale(value_matrix):
    return lax.rsqrt(lax.optimization_barrier(jnp.mean(value_matrix * value_matrix, axis=-1, keepdims=True)) + epsilon)

def rope_angles(positions, head_size):
    frequency = jnp.exp(jnp.arange(0, head_size, 2, dtype=jnp.float32) * (-math.log(rope_base) / head_size))
    return positions.astype(jnp.float32)[:, None] * frequency[None, :]

def apply_rotary(value_matrix, rotary_angles):
    middle_cut = value_matrix.shape[-1] // 2
    former = value_matrix[..., :middle_cut]
    latter = value_matrix[..., middle_cut:]
    cosine = jnp.cos(rotary_angles)[:, None, :]
    sine_part = jnp.sin(rotary_angles)[:, None, :]
    return jnp.concatenate([former * cosine - latter * sine_part, latter * cosine + former * sine_part], axis=-1)

def forward(inputs_wide, gain_one, query_w, key_w, value_weight, out_w, gain_two, gate_w, up_w, down_w, positions, first_token):
    repeat_heads = QUERY_HEADS // KEY_VALUE_HEADS
    score_scale = 1.0 / math.sqrt(HEAD_DIM)
    first_normed = reduced_precision(inputs_wide * rms_scale(inputs_wide) * gain_one)
    query_raw = reduced_precision_back(matrix_multiply(first_normed, query_w))
    key_unrotated = reduced_precision_back(matrix_multiply(first_normed, key_w))
    value_matrix = reduced_precision(reduced_precision_back(matrix_multiply(first_normed, value_weight))).reshape(TOKEN_COUNT, KEY_VALUE_HEADS, HEAD_DIM)
    rotary_angles = rope_angles(positions, HEAD_DIM)
    queries = reduced_precision(apply_rotary(query_raw.reshape(TOKEN_COUNT, QUERY_HEADS, HEAD_DIM), rotary_angles))
    key_matrix = reduced_precision(apply_rotary(key_unrotated.reshape(TOKEN_COUNT, KEY_VALUE_HEADS, HEAD_DIM), rotary_angles))
    key_with_padding = jnp.concatenate([jnp.zeros((SEQUENCE_LENGTH, KEY_VALUE_HEADS, HEAD_DIM), jnp.float32), key_matrix], axis=0)
    value_with_padding = jnp.concatenate([jnp.zeros((SEQUENCE_LENGTH, KEY_VALUE_HEADS, HEAD_DIM), jnp.float32), value_matrix], axis=0)
    query_tile_block = math.gcd(TOKEN_COUNT, 512)

    def block_attend(block_start):
        query_row_set = lax.dynamic_slice_in_dim(queries, block_start, query_tile_block, 0)
        key_rows = lax.dynamic_slice_in_dim(key_with_padding, block_start, query_tile_block + SEQUENCE_LENGTH, 0)
        value_rows = lax.dynamic_slice_in_dim(value_with_padding, block_start, query_tile_block + SEQUENCE_LENGTH, 0)
        query_index = block_start + jnp.arange(query_tile_block, dtype=jnp.int32)
        key_index = block_start - SEQUENCE_LENGTH + jnp.arange(query_tile_block + SEQUENCE_LENGTH, dtype=jnp.int32)
        first_rows = lax.dynamic_slice_in_dim(first_token, block_start, query_tile_block, 0)
        visible = (key_index[None, :] <= query_index[:, None]) & (key_index[None, :] >= first_rows[:, None])
        heads_grouped = query_row_set.reshape(query_tile_block, KEY_VALUE_HEADS, repeat_heads, HEAD_DIM)
        scores = jnp.einsum('bcrd,kcd->crbk', heads_grouped, key_rows, precision=highest) * score_scale
        scores = reduced_precision_back(jnp.where(visible, scores, masked_score))
        probs = reduced_precision(jax.nn.softmax(scores, axis=-1))
        mixed = jnp.einsum('crbk,kcd->bcrd', probs, value_rows, precision=highest)
        return mixed.reshape(query_tile_block, QUERY_HEADS * HEAD_DIM)
    block_starts = jnp.arange(TOKEN_COUNT // query_tile_block, dtype=jnp.int32) * query_tile_block
    attended = lax.map(jax.checkpoint(block_attend), block_starts).reshape(TOKEN_COUNT, QUERY_HEADS * HEAD_DIM)
    attended = reduced_precision(reduced_precision_back(attended))
    middle = inputs_wide + reduced_precision_back(matrix_multiply(attended, out_w))
    feed_rows = math.gcd(TOKEN_COUNT, 4096)

    def feed(rows):
        normed_two = reduced_precision(rows * rms_scale(rows) * gain_two)
        gate = reduced_precision_back(matrix_multiply(normed_two, gate_w))
        upper = reduced_precision_back(matrix_multiply(normed_two, up_w))
        hidden = reduced_precision(jax.nn.silu(gate) * upper)
        return rows + matrix_multiply(hidden, down_w)
    return lax.map(jax.checkpoint(feed), middle.reshape(TOKEN_COUNT // feed_rows, feed_rows, D)).reshape(TOKEN_COUNT, D)

def reference(inputs, seg_ids, seq_starts, gain_one, query_w, key_w, value_weight, out_w, gain_two, gate_w, up_w, down_w, out_grad):
    token_index = jnp.arange(TOKEN_COUNT, dtype=jnp.int32)
    first_token = seq_starts[seg_ids].astype(jnp.int32)
    positions = token_index - first_token

    def wrapped(inputs_wide, g_one, w_query, w_key, w_value, w_out, g_two, w_gate, w_up, w_down):
        return forward(inputs_wide, g_one, w_query, w_key, w_value, w_out, g_two, w_gate, w_up, w_down, positions, first_token)
    primals = tuple((item.astype(jnp.float32) for item in (inputs, gain_one, query_w, key_w, value_weight, out_w, gain_two, gate_w, up_w, down_w)))
    outputs, pullback = jax.vjp(wrapped, *primals)
    grads = pullback(out_grad.astype(jnp.float32))
    return (outputs, grads[0], grads[1], grads[2], grads[3], grads[4], grads[5], grads[6], grads[7], grads[8], grads[9])
```

```python
import functools
import math

import jax
import jax.numpy as jnp
from jax import lax
from jax.experimental import pallas as pl
from jax.experimental.pallas import tpu as pltpu
from jax.sharding import PartitionSpec as P

HEAD_DIM = 64
SEQUENCE_LENGTH = 2048


epsilon = 1e-05
rope_base = 100000.0
masked_score = -1e30


def from_behind(block, axis, distance):
    devices = range(lax.axis_size(axis))
    route = [(i - distance, i) for i in devices if i - distance in devices]
    return lax.ppermute(block, axis, route)


def rms_scale(value_matrix):
    return lax.rsqrt(jnp.mean(value_matrix * value_matrix, axis=-1, keepdims=True) + epsilon)


def rope_angles(positions, head_size):
    frequency = jnp.exp(
        jnp.arange(0, head_size, 2, dtype=jnp.float32) * (-math.log(rope_base) / head_size)
    )
    return positions.astype(jnp.float32)[:, None] * frequency[None, :]


def apply_rotary(value_matrix, rotary_angles):
    middle_cut = value_matrix.shape[-1] // 2
    former = value_matrix[..., :middle_cut]
    latter = value_matrix[..., middle_cut:]
    cosine = jnp.cos(rotary_angles)[:, None, :]
    sine_part = jnp.sin(rotary_angles)[:, None, :]
    return jnp.concatenate(
        [former * cosine - latter * sine_part, latter * cosine + former * sine_part], axis=-1
    )


def contract_rows(former, latter):
    return lax.dot_general(
        former, latter, (((0,), (0,)), ((), ())), preferred_element_type=jnp.float32
    )


def times_transpose(former, latter):
    return lax.dot_general(
        former, latter, (((1,), (1,)), ((), ())), preferred_element_type=jnp.float32
    )


def norm_back(grad_normed, value_matrix, scale_rows, gain_wide):
    weighted = grad_normed * gain_wide
    cubed = scale_rows * scale_rows * scale_rows
    grad_values = scale_rows * weighted - value_matrix * cubed * jnp.mean(
        weighted * value_matrix, axis=-1, keepdims=True
    )
    grad_gain = jnp.sum(grad_normed * value_matrix * scale_rows, axis=0)
    return (grad_values, grad_gain)


MESH = pl.DeviceIdType.MESH
VMEM_LIMIT = 56 * 1024 * 1024


def flip_bit(index, bit):
    return index + bit - 2 * bit * (lax.rem(lax.div(index, bit), 2))


def greet(partners):
    barrier = pltpu.get_barrier_semaphore()
    for partner in partners:
        pl.semaphore_signal(barrier, inc=1, device_id=partner, device_id_type=MESH)
    pl.semaphore_wait(barrier, len(partners))


def remote(source, target, send_sem, recv_sem, partner):
    return pltpu.make_async_remote_copy(
        src_ref=source,
        dst_ref=target,
        send_sem=send_sem,
        recv_sem=recv_sem,
        device_id=partner,
        device_id_type=MESH,
    )


def gather_kernel(qkvo, gate, up, down, qkvo_all, gate_all, up_all, down_all, sends, recvs, local):
    r = lax.axis_index("replica")
    g = lax.axis_index("group")
    core_partner = (r, flip_bit(g, 1))
    y_partner = (r, flip_bit(g, 2))
    x_partner = (flip_bit(r, 1), g)
    x = lax.rem(r, 2)
    across = flip_bit(g, 2)
    greet((core_partner, y_partner, x_partner))
    shards = (qkvo, gate, up, down)
    wholes = (qkvo_all, gate_all, up_all, down_all)

    def half(whole, owner, part):
        if whole.shape[2] % 256 == 0:
            width = whole.shape[2] // 2
            return whole.at[owner, :, pl.ds(pl.multiple_of(part * width, 128), width)]
        height = whole.shape[1] // 2
        return whole.at[owner, pl.ds(pl.multiple_of(part * height, 16), height), :]

    def half_shard(shard, part):
        if shard.shape[1] % 256 == 0:
            width = shard.shape[1] // 2
            return shard.at[:, pl.ds(pl.multiple_of(part * width, 128), width)]
        height = shard.shape[0] // 2
        return shard.at[pl.ds(pl.multiple_of(part * height, 16), height), :]

    started = []
    locals_started = []
    y_copies = []
    for i in range(4):
        copy = remote(
            half_shard(shards[i], x), half(wholes[i], g, x), sends.at[i, 0], recvs.at[i, 0], y_partner
        )
        copy.start()
        y_copies.append(copy)
    core_copies = []
    for i in range(4):
        copy = remote(
            shards[i], wholes[i].at[g], sends.at[i, 1], recvs.at[i, 1], core_partner
        )
        copy.start()
        core_copies.append(copy)
        own = pltpu.make_async_copy(shards[i], wholes[i].at[g], local.at[i])
        own.start()
        locals_started.append(own)
    x_copies = []
    for i in range(4):
        y_copies[i].wait_recv()
        piece = half(wholes[i], across, x)
        copy = remote(piece, piece, sends.at[i, 2], recvs.at[i, 2], x_partner)
        copy.start()
        x_copies.append(copy)
        copy = remote(piece, piece, sends.at[i, 3], recvs.at[i, 3], core_partner)
        copy.start()
        started.append(copy)
    for i in range(4):
        x_copies[i].wait_recv()
        piece = half(wholes[i], across, 1 - x)
        copy = remote(piece, piece, sends.at[i, 4], recvs.at[i, 4], core_partner)
        copy.start()
        started.append(copy)
    for copy in locals_started:
        copy.wait()
    for copy in core_copies:
        copy.wait()
    for copy in started:
        copy.wait()
    for copy in y_copies + x_copies:
        copy.wait_send()


def gather_weights(qkvo, gate, up, down):
    vmem = pl.BlockSpec(memory_space=pltpu.VMEM)
    arrays = (qkvo, gate, up, down)
    return pl.pallas_call(
        gather_kernel,
        out_shape=[jax.ShapeDtypeStruct((4,) + a.shape, a.dtype) for a in arrays],
        in_specs=[vmem] * 4,
        out_specs=[vmem] * 4,
        scratch_shapes=[
            pltpu.SemaphoreType.DMA((4, 5)),
            pltpu.SemaphoreType.DMA((4, 5)),
            pltpu.SemaphoreType.DMA((4,)),
        ],
        compiler_params=pltpu.CompilerParams(
            collective_id=1, has_side_effects=True, vmem_limit_bytes=VMEM_LIMIT
        ),
    )(*arrays)


def ring_partner(offset):
    groups = lax.axis_size("group")
    total = lax.axis_size("replica") * groups
    here = lax.axis_index("replica") * groups + lax.axis_index("group")
    there = lax.rem(here + offset + total, total)
    return (lax.div(there, groups), lax.rem(there, groups))


def window_kernel(reach, packed, window, sends, recvs, local):
    barrier = pltpu.get_barrier_semaphore()
    for offset in range(1, reach + 1):
        pl.semaphore_signal(barrier, inc=1, device_id=ring_partner(-offset), device_id_type=MESH)
    pl.semaphore_wait(barrier, reach)
    copies = []
    for offset in range(reach, 0, -1):
        copy = remote(
            packed,
            window.at[reach - offset],
            sends.at[offset - 1],
            recvs.at[offset - 1],
            ring_partner(offset),
        )
        copy.start()
        copies.append(copy)
    own = pltpu.make_async_copy(packed, window.at[reach], local)
    own.start()
    own.wait()
    for copy in copies:
        copy.wait()


def exchange_window(packed, reach):
    vmem = pl.BlockSpec(memory_space=pltpu.VMEM)
    return pl.pallas_call(
        functools.partial(window_kernel, reach),
        out_shape=jax.ShapeDtypeStruct((reach + 1,) + packed.shape, packed.dtype),
        in_specs=[vmem],
        out_specs=vmem,
        scratch_shapes=[
            pltpu.SemaphoreType.DMA((reach,)),
            pltpu.SemaphoreType.DMA((reach,)),
            pltpu.SemaphoreType.DMA,
        ],
        compiler_params=pltpu.CompilerParams(
            collective_id=2, has_side_effects=True, vmem_limit_bytes=VMEM_LIMIT
        ),
    )(packed)


def return_kernel(reach, window, own, total, landed, sends, recvs):
    barrier = pltpu.get_barrier_semaphore()
    for offset in range(1, reach + 1):
        pl.semaphore_signal(barrier, inc=1, device_id=ring_partner(offset), device_id_type=MESH)
    pl.semaphore_wait(barrier, reach)
    copies = []
    for offset in range(reach, 0, -1):
        copy = remote(
            window.at[reach - offset],
            landed.at[offset - 1],
            sends.at[offset - 1],
            recvs.at[offset - 1],
            ring_partner(-offset),
        )
        copy.start()
        copies.append(copy)
    for copy in copies:
        copy.wait()
    tally = own[...]
    for offset in range(reach):
        tally = tally + landed[offset].astype(jnp.float32)
    total[...] = tally


def return_window(window, own):
    reach = window.shape[0]
    vmem = pl.BlockSpec(memory_space=pltpu.VMEM)
    return pl.pallas_call(
        functools.partial(return_kernel, reach),
        out_shape=jax.ShapeDtypeStruct(own.shape, jnp.float32),
        in_specs=[vmem, vmem],
        out_specs=vmem,
        scratch_shapes=[
            pltpu.VMEM(window.shape, window.dtype),
            pltpu.SemaphoreType.DMA((reach,)),
            pltpu.SemaphoreType.DMA((reach,)),
        ],
        compiler_params=pltpu.CompilerParams(
            collective_id=3, has_side_effects=True, vmem_limit_bytes=VMEM_LIMIT
        ),
    )(window, own)


CHUNKS = 3
TILES = 16


def reduce_kernel(
    replicas,
    normed_two_t,
    normed_one_t,
    attended_t,
    out_grad_t,
    grad_gate,
    grad_up,
    grad_qkvo,
    hidden,
    gains,
    out_wide,
    out_down,
    out_gains,
    parts,
    from_core,
    from_y,
    from_x,
    from_z,
    from_far,
    final,
    tally,
    from_gain,
    sends,
    recvs,
    gain_sends,
    gain_recvs,
):
    r = lax.axis_index("replica")
    g = lax.axis_index("group")
    c = lax.rem(g, 2)
    y = lax.div(g, 2)
    x = lax.rem(r, 2)
    z = lax.rem(lax.div(r, 2), 4)
    base = r - 2 * z
    core_partner = (r, flip_bit(g, 1))
    y_partner = (r, flip_bit(g, 2))
    x_partner = (flip_bit(r, 1), g)
    z_partners = [(base + 2 * lax.rem(z + d, 4), g) for d in (1, 2, 3)]
    far_bits = []
    bit = 8
    while bit < replicas:
        far_bits.append(bit)
        bit *= 2
    far_partners = [(flip_bit(r, bit), g) for bit in far_bits]
    greet([core_partner, y_partner, x_partner] + z_partners + far_partners)
    half = TILES // 2
    piece = TILES // 8
    lefts = (normed_two_t, normed_two_t, normed_one_t)
    rights = (grad_gate, grad_up, grad_qkvo)
    pending = []

    def start(chunk, slot, source, target, partner):
        copy = remote(source, target, sends.at[chunk, slot], recvs.at[chunk, slot], partner)
        copy.start()
        pending.append(copy)
        return copy

    gain_slot = [0]

    def gain_start(target, partner):
        slot = gain_slot[0]
        gain_slot[0] += 1
        copy = remote(tally.at[target], from_gain.at[slot], gain_sends.at[slot], gain_recvs.at[slot], partner)
        copy.start()
        pending.append(copy)
        return (copy, slot)

    def stage_product(k):
        for pair in range(6):
            columns = slice(pair * 256, pair * 256 + 256)
            right = rights[k][:, columns]
            if k == 2 and pair >= 4:
                product = jnp.dot(attended_t[...], right, preferred_element_type=jnp.float32)
            else:
                product = jnp.dot(lefts[k][...], right, preferred_element_type=jnp.float32)
            if k == 2 and pair == 3:
                other = jnp.dot(attended_t[...], right, preferred_element_type=jnp.float32)
                lane = lax.broadcasted_iota(jnp.int32, product.shape, 1)
                product = jnp.where(lane < 960 - 768, product, other)
            product = product.astype(jnp.bfloat16)
            for s in range(4):
                rows = product[144 * s : 144 * s + 144]
                parts[s % 2, s // 2, k, 2 * pair] = rows[:, :128]
                parts[s % 2, s // 2, k, 2 * pair + 1] = rows[:, 128:]
        for s in range(4):
            columns = slice(s * 384 + k * 128, s * 384 + k * 128 + 128)
            product = jnp.dot(
                out_grad_t[...], hidden[:, columns], preferred_element_type=jnp.float32
            ).astype(jnp.bfloat16)
            for row in range(4):
                parts[s % 2, s // 2, k, 12 + row] = product[144 * row : 144 * row + 144]
        return start(k, 0, parts.at[1 - c, :, k], from_core.at[k], core_partner)

    def stage_y(k, arrived):
        arrived.wait_recv()

        def add(t, carry):
            for yy in range(2):
                parts[c, yy, k, t] = (
                    parts[c, yy, k, t].astype(jnp.float32) + from_core[k, yy, t].astype(jnp.float32)
                ).astype(jnp.bfloat16)
            return carry

        lax.fori_loop(0, TILES, add, 0)
        return start(k, 1, parts.at[c, 1 - y, k], from_y.at[k], y_partner)

    def stage_x(k, arrived):
        arrived.wait_recv()

        def add(t, carry):
            parts[c, y, k, t] = (
                parts[c, y, k, t].astype(jnp.float32) + from_y[k, t].astype(jnp.float32)
            ).astype(jnp.bfloat16)
            return carry

        lax.fori_loop(0, TILES, add, 0)
        return start(
            k, 2, parts.at[c, y, k, pl.ds((1 - x) * half, half)], from_x.at[k], x_partner
        )

    def stage_z(k, arrived):
        arrived.wait_recv()

        def add(t, carry):
            parts[c, y, k, x * half + t] = (
                parts[c, y, k, x * half + t].astype(jnp.float32) + from_x[k, t].astype(jnp.float32)
            ).astype(jnp.bfloat16)
            return carry

        lax.fori_loop(0, half, add, 0)
        copies = []
        for d in range(1, 4):
            there = lax.rem(z + d, 4)
            copies.append(
                start(
                    k,
                    2 + d,
                    parts.at[c, y, k, pl.ds(x * half + there * piece, piece)],
                    from_z.at[k, d - 1],
                    z_partners[d - 1],
                )
            )
        return copies

    def stage_back(k, arrived):
        for copy in arrived:
            copy.wait_recv()
        spot = x * half + z * piece
        for t in range(piece):
            total = parts[c, y, k, spot + t].astype(jnp.float32)
            for d in range(3):
                total = total + from_z[k, d, t].astype(jnp.float32)
            final[k, spot + t] = total.astype(jnp.bfloat16)
        for step in range(len(far_bits)):
            from_far[k, 2 * step] = final[k, pl.ds(spot, piece)]
            copy = start(
                k,
                9 + step,
                from_far.at[k, 2 * step],
                from_far.at[k, 2 * step + 1],
                far_partners[step],
            )
            copy.wait_recv()
            for t in range(piece):
                final[k, spot + t] = (
                    final[k, spot + t].astype(jnp.float32)
                    + from_far[k, 2 * step + 1, t].astype(jnp.float32)
                ).astype(jnp.bfloat16)
        own = final.at[k, pl.ds(spot, piece)]
        return [start(k, 5 + d, own, own, z_partners[d - 1]) for d in range(1, 4)]

    def stage_back_x(k, arrived):
        for copy in arrived:
            copy.wait_recv()
        own = final.at[k, pl.ds(x * half, half)]
        return start(k, 9 + len(far_bits), own, own, x_partner)

    def stage_out(k, arrived):
        arrived.wait_recv()
        for t in range(12):
            out_wide[k, :, t * 128 : t * 128 + 128] = final[k, t].astype(jnp.float32)
        column = jnp.concatenate(
            [final[k, 12 + row].astype(jnp.float32) for row in range(4)], axis=0
        )
        out_down[k * 128 : k * 128 + 128, :] = column.T

    stages = (stage_product, stage_y, stage_x, stage_z, stage_back, stage_back_x, stage_out)
    state = [None] * CHUNKS

    gain_steps = [[core_partner], [y_partner], [x_partner], z_partners] + [[p] for p in far_partners]
    tally[0] = gains[...]
    gain_flight = []
    for t in range(CHUNKS + len(stages) - 1):
        for k in range(CHUNKS):
            s = t - k
            if s == 0:
                state[k] = stage_product(k)
            elif 0 < s < len(stages):
                state[k] = stages[s](k, state[k])
        if t <= len(gain_steps):
            if gain_flight:
                total = tally[t - 1]
                for copy, slot in gain_flight:
                    copy.wait_recv()
                    total = total + from_gain[slot]
                if t < len(gain_steps):
                    tally[t] = total
                else:
                    out_gains[...] = total
                gain_flight = []
            if t < len(gain_steps):
                gain_flight = [gain_start(t, p) for p in gain_steps[t]]
    for copy in pending:
        copy.wait_send()


def reduce_gradients(replicas, *operands):
    vmem = pl.BlockSpec(memory_space=pltpu.VMEM)
    far = max(replicas.bit_length() - 4, 0)
    slots = 10 + far
    gain_slots = 6 + far
    tile = (144, 128)
    low = jnp.bfloat16
    return pl.pallas_call(
        functools.partial(reduce_kernel, replicas),
        out_shape=[
            jax.ShapeDtypeStruct((CHUNKS, 144, 1536), jnp.float32),
            jax.ShapeDtypeStruct((384, 576), jnp.float32),
            jax.ShapeDtypeStruct((8, 256), jnp.float32),
        ],
        in_specs=[vmem] * 9,
        out_specs=[vmem] * 3,
        scratch_shapes=[
            pltpu.VMEM((2, 2, CHUNKS, TILES) + tile, low),
            pltpu.VMEM((CHUNKS, 2, TILES) + tile, low),
            pltpu.VMEM((CHUNKS, TILES) + tile, low),
            pltpu.VMEM((CHUNKS, TILES // 2) + tile, low),
            pltpu.VMEM((CHUNKS, 3, TILES // 8) + tile, low),
            pltpu.VMEM((CHUNKS, 2 * max(far, 1), TILES // 8) + tile, low),
            pltpu.VMEM((CHUNKS, TILES) + tile, low),
            pltpu.VMEM((4 + far, 8, 256), jnp.float32),
            pltpu.VMEM((gain_slots, 8, 256), jnp.float32),
            pltpu.SemaphoreType.DMA((CHUNKS, slots)),
            pltpu.SemaphoreType.DMA((CHUNKS, slots)),
            pltpu.SemaphoreType.DMA((gain_slots,)),
            pltpu.SemaphoreType.DMA((gain_slots,)),
        ],
        compiler_params=pltpu.CompilerParams(
            collective_id=4, has_side_effects=True, vmem_limit_bytes=VMEM_LIMIT
        ),
    )(*operands)


def per_device(
    inputs,
    seg_ids,
    seq_starts,
    gain_one,
    query_w,
    key_w,
    value_weight,
    out_w,
    gain_two,
    gate_w,
    up_w,
    down_w,
    out_grad,
):
    qkvo_all, gate_all, up_all, down_all = gather_weights(
        jnp.concatenate([query_w, key_w, value_weight, out_w], axis=1), gate_w, up_w, down_w
    )
    qkvo_all, gate_all, up_all, down_all = (
        a.reshape(a.shape[0] * a.shape[1], a.shape[2]) for a in (qkvo_all, gate_all, up_all, down_all)
    )
    joined_w = qkvo_all[:, : query_w.shape[1] + 2 * key_w.shape[1]]
    out_all = qkvo_all[:, query_w.shape[1] + 2 * key_w.shape[1] :]
    query_all = qkvo_all[:, : query_w.shape[1]]
    key_all = qkvo_all[:, query_w.shape[1] : query_w.shape[1] + key_w.shape[1]]
    gain_one_all = lax.all_gather(gain_one, "group", axis=0, tiled=True)
    gain_two_all = lax.all_gather(gain_two, "group", axis=0, tiled=True)
    tok_rows = inputs.shape[0]
    query_heads = query_all.shape[1] // HEAD_DIM
    kv_heads = key_all.shape[1] // HEAD_DIM
    repeat_heads = query_heads // kv_heads
    kv_width = kv_heads * HEAD_DIM
    score_scale = 1.0 / math.sqrt(HEAD_DIM)
    reach_back = SEQUENCE_LENGTH // tok_rows
    window_rows = (reach_back + 1) * tok_rows
    device = lax.axis_index(("replica", "group"))
    token_index = device * tok_rows + jnp.arange(tok_rows, dtype=jnp.int32)
    segment_table = jnp.arange(seq_starts.shape[0], dtype=jnp.int32)
    first_token = jnp.sum(
        jnp.where(seg_ids[:, None] == segment_table[None, :], seq_starts[None, :], 0), axis=1
    )
    rotary_angles = rope_angles(token_index - first_token, HEAD_DIM)
    key_index = (device - reach_back) * tok_rows + jnp.arange(window_rows, dtype=jnp.int32)
    visible = (key_index[None, :] <= token_index[:, None]) & (
        key_index[None, :] >= first_token[:, None]
    )
    inputs_wide = inputs.astype(jnp.float32)
    scale_one = rms_scale(inputs_wide)
    gain_one_wide = gain_one_all.astype(jnp.float32)
    first_normed = (inputs_wide * scale_one * gain_one_wide).astype(jnp.bfloat16)
    projected = jnp.dot(first_normed, joined_w, preferred_element_type=jnp.float32)
    query_cols = query_heads * HEAD_DIM
    queries = apply_rotary(
        projected[:, :query_cols].reshape(tok_rows, query_heads, HEAD_DIM), rotary_angles
    ).astype(jnp.bfloat16)
    key_matrix = apply_rotary(
        projected[:, query_cols : query_cols + kv_width].reshape(tok_rows, kv_heads, HEAD_DIM),
        rotary_angles,
    )
    key_matrix = key_matrix.astype(jnp.bfloat16).reshape(tok_rows, kv_width)
    value_matrix = projected[:, query_cols + kv_width :].astype(jnp.bfloat16)
    packed = jnp.concatenate([key_matrix, value_matrix], axis=1)
    window = exchange_window(packed, reach_back).reshape(window_rows, 2 * kv_width)
    key_grid = window[:, :kv_width].reshape(window_rows, kv_heads, HEAD_DIM)
    value_grid = window[:, kv_width:].reshape(window_rows, kv_heads, HEAD_DIM)
    query_grid = queries.reshape(tok_rows, kv_heads, repeat_heads, HEAD_DIM)

    def masked_scores():
        raw_scores = (
            jnp.einsum("tcrd,wcd->crtw", query_grid, key_grid, preferred_element_type=jnp.float32)
            * score_scale
        )
        return jnp.where(visible, raw_scores, masked_score)

    scores = masked_scores()
    row_peak = jnp.max(scores, axis=-1, keepdims=True)
    exponent = jnp.exp(scores - row_peak)
    row_total = jnp.sum(exponent, axis=-1, keepdims=True)
    log_total = row_peak + jnp.log(row_total)
    probs_low = (exponent / row_total).astype(jnp.bfloat16)
    attended = jnp.einsum(
        "crtw,wcd->tcrd", probs_low, value_grid, preferred_element_type=jnp.float32
    )
    attended = attended.reshape(tok_rows, query_cols).astype(jnp.bfloat16)
    middle = inputs_wide + jnp.dot(attended, out_all, preferred_element_type=jnp.float32)
    scale_two = rms_scale(middle)
    gain_two_wide = gain_two_all.astype(jnp.float32)
    normed_two = (middle * scale_two * gain_two_wide).astype(jnp.bfloat16)
    gate = jnp.dot(normed_two, gate_all, preferred_element_type=jnp.float32)
    upper = jnp.dot(normed_two, up_all, preferred_element_type=jnp.float32)
    sigmoid_gate = jax.nn.sigmoid(gate)
    hidden = (gate * sigmoid_gate * upper).astype(jnp.bfloat16)
    outputs = middle + jnp.dot(hidden, down_all, preferred_element_type=jnp.float32)
    grad_hidden = times_transpose(out_grad, down_all)
    grad_gate = (grad_hidden * upper * sigmoid_gate * (1.0 + gate * (1.0 - sigmoid_gate))).astype(
        jnp.bfloat16
    )
    grad_up = (grad_hidden * gate * sigmoid_gate).astype(jnp.bfloat16)
    grad_normed_two = times_transpose(grad_gate, gate_all) + times_transpose(grad_up, up_all)
    grad_middle_norm, grad_gain_two = norm_back(grad_normed_two, middle, scale_two, gain_two_wide)
    grad_middle = out_grad.astype(jnp.float32) + grad_middle_norm
    grad_branch = grad_middle.astype(jnp.bfloat16)
    grad_attended = (
        times_transpose(grad_branch, out_all)
        .astype(jnp.bfloat16)
        .reshape(tok_rows, kv_heads, repeat_heads, HEAD_DIM)
    )
    scores_again = masked_scores()
    probs = jnp.exp(scores_again - log_total)
    probs_again = probs.astype(jnp.bfloat16)
    grad_probs = jnp.einsum(
        "tcrd,wcd->crtw", grad_attended, value_grid, preferred_element_type=jnp.float32
    )
    inner = jnp.sum(probs * grad_probs, axis=-1, keepdims=True)
    grad_scores = (probs * (grad_probs - inner)).astype(jnp.bfloat16)
    grad_query_rot = (
        jnp.einsum("crtw,wcd->tcrd", grad_scores, key_grid, preferred_element_type=jnp.float32)
        * score_scale
    )
    grad_key_rot = (
        jnp.einsum("crtw,tcrd->wcd", grad_scores, query_grid, preferred_element_type=jnp.float32)
        * score_scale
    )
    grad_value_win = jnp.einsum(
        "crtw,tcrd->wcd", probs_again, grad_attended, preferred_element_type=jnp.float32
    )
    grad_window = jnp.concatenate(
        [
            grad_key_rot.reshape(window_rows, kv_width),
            grad_value_win.reshape(window_rows, kv_width),
        ],
        axis=1,
    )
    own_grad = return_window(
        grad_window[: reach_back * tok_rows]
        .astype(jnp.bfloat16)
        .reshape(reach_back, tok_rows, 2 * kv_width),
        grad_window[reach_back * tok_rows :],
    )
    grad_keys = apply_rotary(
        own_grad[:, :kv_width].reshape(tok_rows, kv_heads, HEAD_DIM), -rotary_angles
    )
    grad_keys = grad_keys.reshape(tok_rows, kv_width).astype(jnp.bfloat16)
    grad_values = own_grad[:, kv_width:].astype(jnp.bfloat16)
    grad_queries = apply_rotary(
        grad_query_rot.reshape(tok_rows, query_heads, HEAD_DIM), -rotary_angles
    )
    grad_queries = grad_queries.reshape(tok_rows, query_cols).astype(jnp.bfloat16)
    grad_qkv = jnp.concatenate([grad_queries, grad_keys, grad_values], axis=1)
    grad_normed_one = times_transpose(grad_qkv, joined_w)
    grad_inputs_norm, grad_gain_one = norm_back(
        grad_normed_one, inputs_wide, scale_one, gain_one_wide
    )
    grad_inputs = grad_middle + grad_inputs_norm
    width = gain_one_all.shape[0]
    gain_grads = jnp.pad(jnp.concatenate([grad_gain_one, grad_gain_two]), (0, 2048 - 2 * width))
    wide, grad_down_w, gain_sums = reduce_gradients(
        lax.axis_size("replica"),
        normed_two.T,
        first_normed.T,
        attended.T,
        out_grad.T,
        grad_gate,
        grad_up,
        jnp.concatenate([grad_qkv, grad_branch], axis=1),
        hidden,
        gain_grads.reshape(8, 256),
    )
    gain_sums = gain_sums.reshape(2048)[: 2 * width].reshape(2, width)
    shard = width // lax.axis_size("group")
    gain_sums = lax.dynamic_slice_in_dim(gain_sums, lax.axis_index("group") * shard, shard, 1)
    first = query_cols
    second = first + kv_width
    third = second + kv_width
    return (
        outputs,
        grad_inputs,
        gain_sums[0],
        wide[2, :, :first],
        wide[2, :, first:second],
        wide[2, :, second:third],
        wide[2, :, third:],
        gain_sums[1],
        wide[0],
        wide[1],
        grad_down_w,
    )


def solution(mesh):
    placed = (
        P(("replica", "group"), None),
        P(("replica", "group")),
        P(),
        P("group"),
        P("group", None),
        P("group", None),
        P("group", None),
        P("group", None),
        P("group"),
        P("group", None),
        P("group", None),
        P("group", None),
        P(("replica", "group"), None),
    )
    return jax.shard_map(
        per_device,
        mesh=mesh,
        in_specs=placed,
        out_specs=(
            P(("replica", "group"), None),
            P(("replica", "group"), None),
            P("group"),
            P("group", None),
            P("group", None),
            P("group", None),
            P("group", None),
            P("group"),
            P("group", None),
            P("group", None),
            P("group", None),
        ),
        check_vma=False,
    )
```

```python
import functools
import math

import jax
import jax.numpy as jnp
from jax import lax
from jax.experimental import pallas as pl
from jax.experimental.pallas import tpu as pltpu
from jax.sharding import PartitionSpec as P

HEAD_DIM = 64
SEQUENCE_LENGTH = 2048


epsilon = 1e-05
rope_base = 100000.0
masked_score = -1e30


def from_behind(block, axis, distance):
    devices = range(lax.axis_size(axis))
    route = [(i - distance, i) for i in devices if i - distance in devices]
    return lax.ppermute(block, axis, route)


def rms_scale(value_matrix):
    return lax.rsqrt(jnp.mean(value_matrix * value_matrix, axis=-1, keepdims=True) + epsilon)


def rope_angles(positions, head_size):
    frequency = jnp.exp(
        jnp.arange(0, head_size, 2, dtype=jnp.float32) * (-math.log(rope_base) / head_size)
    )
    return positions.astype(jnp.float32)[:, None] * frequency[None, :]


def apply_rotary(value_matrix, rotary_angles):
    middle_cut = value_matrix.shape[-1] // 2
    former = value_matrix[..., :middle_cut]
    latter = value_matrix[..., middle_cut:]
    cosine = jnp.cos(rotary_angles)[:, None, :]
    sine_part = jnp.sin(rotary_angles)[:, None, :]
    return jnp.concatenate(
        [former * cosine - latter * sine_part, latter * cosine + former * sine_part], axis=-1
    )


def contract_rows(former, latter):
    return lax.dot_general(
        former, latter, (((0,), (0,)), ((), ())), preferred_element_type=jnp.float32
    )


def times_transpose(former, latter):
    return lax.dot_general(
        former, latter, (((1,), (1,)), ((), ())), preferred_element_type=jnp.float32
    )


def norm_back(grad_normed, value_matrix, scale_rows, gain_wide):
    weighted = grad_normed * gain_wide
    cubed = scale_rows * scale_rows * scale_rows
    grad_values = scale_rows * weighted - value_matrix * cubed * jnp.mean(
        weighted * value_matrix, axis=-1, keepdims=True
    )
    grad_gain = jnp.sum(grad_normed * value_matrix * scale_rows, axis=0)
    return (grad_values, grad_gain)


MESH = pl.DeviceIdType.MESH
VMEM_LIMIT = 56 * 1024 * 1024


def flip_bit(index, bit):
    return index + bit - 2 * bit * (lax.rem(lax.div(index, bit), 2))


def greet(partners):
    barrier = pltpu.get_barrier_semaphore()
    for partner in partners:
        pl.semaphore_signal(barrier, inc=1, device_id=partner, device_id_type=MESH)
    pl.semaphore_wait(barrier, len(partners))


def remote(source, target, send_sem, recv_sem, partner):
    return pltpu.make_async_remote_copy(
        src_ref=source,
        dst_ref=target,
        send_sem=send_sem,
        recv_sem=recv_sem,
        device_id=partner,
        device_id_type=MESH,
    )


def gather_kernel(qkvo, gate, up, down, qkvo_all, gate_all, up_all, down_all, sends, recvs, local):
    r = lax.axis_index("replica")
    g = lax.axis_index("group")
    core_partner = (r, flip_bit(g, 1))
    y_partner = (r, flip_bit(g, 2))
    x_partner = (flip_bit(r, 1), g)
    x = lax.rem(r, 2)
    across = flip_bit(g, 2)
    greet((core_partner, y_partner, x_partner))
    shards = (qkvo, gate, up, down)
    wholes = (qkvo_all, gate_all, up_all, down_all)

    def half(whole, owner, part):
        if whole.shape[2] % 256 == 0:
            width = whole.shape[2] // 2
            return whole.at[owner, :, pl.ds(pl.multiple_of(part * width, 128), width)]
        height = whole.shape[1] // 2
        return whole.at[owner, pl.ds(pl.multiple_of(part * height, 16), height), :]

    def half_shard(shard, part):
        if shard.shape[1] % 256 == 0:
            width = shard.shape[1] // 2
            return shard.at[:, pl.ds(pl.multiple_of(part * width, 128), width)]
        height = shard.shape[0] // 2
        return shard.at[pl.ds(pl.multiple_of(part * height, 16), height), :]

    started = []
    locals_started = []
    y_copies = []
    for i in range(4):
        copy = remote(
            half_shard(shards[i], x), half(wholes[i], g, x), sends.at[i, 0], recvs.at[i, 0], y_partner
        )
        copy.start()
        y_copies.append(copy)
    core_copies = []
    for i in range(4):
        copy = remote(
            shards[i], wholes[i].at[g], sends.at[i, 1], recvs.at[i, 1], core_partner
        )
        copy.start()
        core_copies.append(copy)
        own = pltpu.make_async_copy(shards[i], wholes[i].at[g], local.at[i])
        own.start()
        locals_started.append(own)
    x_copies = []
    for i in range(4):
        y_copies[i].wait_recv()
        piece = half(wholes[i], across, x)
        copy = remote(piece, piece, sends.at[i, 2], recvs.at[i, 2], x_partner)
        copy.start()
        x_copies.append(copy)
        copy = remote(piece, piece, sends.at[i, 3], recvs.at[i, 3], core_partner)
        copy.start()
        started.append(copy)
    for i in range(4):
        x_copies[i].wait_recv()
        piece = half(wholes[i], across, 1 - x)
        copy = remote(piece, piece, sends.at[i, 4], recvs.at[i, 4], core_partner)
        copy.start()
        started.append(copy)
    for copy in locals_started:
        copy.wait()
    for copy in core_copies:
        copy.wait()
    for copy in started:
        copy.wait()
    for copy in y_copies + x_copies:
        copy.wait_send()


def gather_weights(qkvo, gate, up, down):
    vmem = pl.BlockSpec(memory_space=pltpu.VMEM)
    arrays = (qkvo, gate, up, down)
    return pl.pallas_call(
        gather_kernel,
        out_shape=[jax.ShapeDtypeStruct((4,) + a.shape, a.dtype) for a in arrays],
        in_specs=[vmem] * 4,
        out_specs=[vmem] * 4,
        scratch_shapes=[
            pltpu.SemaphoreType.DMA((4, 5)),
            pltpu.SemaphoreType.DMA((4, 5)),
            pltpu.SemaphoreType.DMA((4,)),
        ],
        compiler_params=pltpu.CompilerParams(
            collective_id=1, has_side_effects=True, vmem_limit_bytes=VMEM_LIMIT
        ),
    )(*arrays)


def place():
    r = lax.axis_index("replica")
    g = lax.axis_index("group")
    slabs = lax.axis_size("replica") // 2
    slab = lax.div(r, 2)
    return r, g, slabs, slab


def slot_of(block, here):
    return lax.rem(block - here + 8, 8)


def window_kernel(packed, window, sends, recvs, local):
    r, g, slabs, slab = place()
    x = lax.rem(r, 2)
    y = lax.div(g, 2)
    c = lax.rem(g, 2)
    rx, gy, gc = flip_bit(r, 1), flip_bit(g, 2), flip_bit(g, 1)
    here = x * 4 + g
    at_x, at_y, at_c = (1 - x) * 4 + g, x * 4 + gy, x * 4 + gc
    at_xy = (1 - x) * 4 + gy
    ahead = (2 * lax.rem(slab + 1, slabs) + x, g)
    behind = (2 * lax.rem(slab + slabs - 1, slabs) + x, g)
    barrier = pltpu.get_barrier_semaphore()
    for partner in ((rx, g), (r, gy), (r, gc), behind):
        pl.semaphore_signal(barrier, inc=1, device_id=partner, device_id_type=MESH)
    pl.semaphore_wait(barrier, 4)
    to_ahead = remote(packed, window.at[0], sends.at[0], recvs.at[0], ahead)
    to_ahead.start()
    firsts = []
    for i, (bit, partner, there) in enumerate(
        ((x, (rx, g), at_x), (y, (r, gy), at_y), (c, (r, gc), at_c))
    ):
        target = window.at[slot_of(here, there)]
        early = remote(packed, target, sends.at[1 + i], recvs.at[1 + i], partner)
        late = remote(window.at[0], target, sends.at[1 + i], recvs.at[1 + i], partner)
        firsts.append((bit, early, late))
    for bit, early, late in firsts:
        pl.when(bit == 0)(early.start)
    own = pltpu.make_async_copy(packed, window.at[8], local)
    own.start()
    to_ahead.wait_recv()
    for bit, early, late in firsts:
        pl.when(bit == 1)(late.start)
    firsts[0][1].wait_recv()
    slot_x = window.at[slot_of(at_x, here)]
    diagonal = remote(
        slot_x, window.at[slot_of(at_x, at_y)], sends.at[4], recvs.at[4], (r, gy)
    )
    diagonal.start()
    core_x = remote(slot_x, window.at[slot_of(at_x, at_c)], sends.at[5], recvs.at[5], (r, gc))
    core_x.start()
    firsts[1][1].wait_recv()
    slot_y = window.at[slot_of(at_y, here)]
    core_y = remote(slot_y, window.at[slot_of(at_y, at_c)], sends.at[6], recvs.at[6], (r, gc))
    core_y.start()
    diagonal.wait_recv()
    slot_xy = window.at[slot_of(at_xy, here)]
    core_xy = remote(slot_xy, window.at[slot_of(at_xy, at_c)], sends.at[7], recvs.at[7], (r, gc))
    core_xy.start()
    firsts[2][1].wait_recv()
    for copy in (core_x, core_y, core_xy):
        copy.wait_recv()
    own.wait()
    for copy in (to_ahead, firsts[0][1], firsts[1][1], firsts[2][1], diagonal, core_x, core_y, core_xy):
        copy.wait_send()


def exchange_window(packed):
    vmem = pl.BlockSpec(memory_space=pltpu.VMEM)
    return pl.pallas_call(
        window_kernel,
        out_shape=jax.ShapeDtypeStruct((9,) + packed.shape, packed.dtype),
        in_specs=[vmem],
        out_specs=vmem,
        scratch_shapes=[
            pltpu.SemaphoreType.DMA((8,)),
            pltpu.SemaphoreType.DMA((8,)),
            pltpu.SemaphoreType.DMA,
        ],
        compiler_params=pltpu.CompilerParams(
            collective_id=2, has_side_effects=True, vmem_limit_bytes=VMEM_LIMIT
        ),
    )(packed)


def return_kernel(window, total, outgoing, landed, sums, sends, recvs):
    r, g, slabs, slab = place()
    x = lax.rem(r, 2)
    y = lax.div(g, 2)
    c = lax.rem(g, 2)
    rx, gy, gc = flip_bit(r, 1), flip_bit(g, 2), flip_bit(g, 1)
    here = x * 4 + g
    at_x, at_y, at_c = (1 - x) * 4 + g, x * 4 + gy, x * 4 + gc
    at_xy = (1 - x) * 4 + gy
    far = [x * 4 + gc, x * 4 + flip_bit(gc, 2), (1 - x) * 4 + gc, (1 - x) * 4 + flip_bit(gc, 2)]
    ahead = (2 * lax.rem(slab + 1, slabs) + x, g)
    behind = (2 * lax.rem(slab + slabs - 1, slabs) + x, g)
    barrier = pltpu.get_barrier_semaphore()
    for partner in ((rx, g), (r, gy), (r, gc), ahead):
        pl.semaphore_signal(barrier, inc=1, device_id=partner, device_id_type=MESH)
    pl.semaphore_wait(barrier, 4)
    wide = jnp.float32
    low = jnp.bfloat16
    core = []
    for i in (3, 1, 2, 0):
        copy = remote(
            window.at[slot_of(far[i], here)], landed.at[i], sends.at[i], recvs.at[i], (r, gc)
        )
        copy.start()
        core.append(copy)

    def blend(bit, index):
        block = landed[index].astype(wide)
        zero = jnp.zeros_like(block)
        total[...] += jnp.where(bit == 0, block, zero)
        sums[...] += jnp.where(bit == 1, block, zero)

    core[0].wait_recv()
    outgoing[0] = (window[slot_of(at_xy, here)].astype(wide) + landed[3].astype(wide)).astype(low)
    to_y_diagonal = remote(outgoing.at[0], landed.at[4], sends.at[4], recvs.at[4], (r, gy))
    to_y_diagonal.start()
    core[1].wait_recv()
    outgoing[1] = (window[slot_of(at_y, here)].astype(wide) + landed[1].astype(wide)).astype(low)
    to_y = remote(outgoing.at[1], landed.at[5], sends.at[5], recvs.at[5], (r, gy))
    to_y.start()
    core[2].wait_recv()
    to_y_diagonal.wait_recv()
    outgoing[2] = (
        window[slot_of(at_x, here)].astype(wide) + landed[2].astype(wide) + landed[4].astype(wide)
    ).astype(low)
    to_x = remote(outgoing.at[2], landed.at[6], sends.at[6], recvs.at[6], (rx, g))
    to_x.start()
    total[...] = window[8].astype(wide)
    sums[...] = window[0].astype(wide)
    core[3].wait_recv()
    blend(c, 0)
    to_y.wait_recv()
    blend(y, 5)
    to_x.wait_recv()
    blend(x, 6)
    outgoing[3] = sums[...].astype(low)
    to_behind = remote(outgoing.at[3], landed.at[7], sends.at[7], recvs.at[7], behind)
    to_behind.start()
    to_behind.wait_recv()
    total[...] += landed[7].astype(wide)
    for copy in core + [to_y_diagonal, to_y, to_x, to_behind]:
        copy.wait_send()


def return_window(window):
    block = window.shape[1:]
    vmem = pl.BlockSpec(memory_space=pltpu.VMEM)
    return pl.pallas_call(
        return_kernel,
        out_shape=jax.ShapeDtypeStruct(block, jnp.float32),
        in_specs=[vmem],
        out_specs=vmem,
        scratch_shapes=[
            pltpu.VMEM((4,) + block, window.dtype),
            pltpu.VMEM((8,) + block, window.dtype),
            pltpu.VMEM(block, jnp.float32),
            pltpu.SemaphoreType.DMA((8,)),
            pltpu.SemaphoreType.DMA((8,)),
        ],
        compiler_params=pltpu.CompilerParams(
            collective_id=3, has_side_effects=True, vmem_limit_bytes=VMEM_LIMIT
        ),
    )(window)


TILES = 8


class Reduction:
    def __init__(self, replicas, chunks, buffers, sends, recvs):
        (
            self.parts,
            self.from_core,
            self.from_y,
            self.from_x,
            self.from_z,
            self.from_far,
            self.final,
        ) = buffers
        self.sends, self.recvs = sends, recvs
        r = lax.axis_index("replica")
        g = lax.axis_index("group")
        self.c, self.y, self.x = lax.rem(g, 2), lax.div(g, 2), lax.rem(r, 2)
        self.z = lax.rem(lax.div(r, 2), 4)
        base = r - 2 * self.z
        self.core_partner = (r, flip_bit(g, 1))
        self.y_partner = (r, flip_bit(g, 2))
        self.x_partner = (flip_bit(r, 1), g)
        self.z_partners = [(base + 2 * lax.rem(self.z + d, 4), g) for d in (1, 2, 3)]
        self.far_partners = []
        bit = 8
        while bit < replicas:
            self.far_partners.append((flip_bit(r, bit), g))
            bit *= 2
        self.pending = []
        self.stages = (
            self.stage_core,
            self.stage_y,
            self.stage_x,
            self.stage_z,
            self.stage_back,
            self.stage_back_x,
            self.stage_end,
        )
        self.state = [None] * chunks

    def greet(self):
        greet(
            [self.core_partner, self.y_partner, self.x_partner] + self.z_partners + self.far_partners
        )

    def advance(self, chunk, stage):
        self.state[chunk] = self.stages[stage](chunk, self.state[chunk])

    def start(self, chunk, slot, source, target, partner):
        copy = remote(source, target, self.sends.at[chunk, slot], self.recvs.at[chunk, slot], partner)
        copy.start()
        self.pending.append(copy)
        return copy

    def finish(self):
        for copy in self.pending:
            copy.wait_send()

    def stage_core(self, k, arrived):
        return self.start(
            k, 0, self.parts.at[1 - self.c, :, k], self.from_core.at[k], self.core_partner
        )

    def stage_y(self, k, arrived):
        arrived.wait_recv()
        parts, c = self.parts, self.c

        def add(t, carry):
            for yy in range(2):
                parts[c, yy, k, t] = (
                    parts[c, yy, k, t].astype(jnp.float32)
                    + self.from_core[k, yy, t].astype(jnp.float32)
                ).astype(jnp.bfloat16)
            return carry

        lax.fori_loop(0, TILES, add, 0)
        return self.start(k, 1, parts.at[c, 1 - self.y, k], self.from_y.at[k], self.y_partner)

    def stage_x(self, k, arrived):
        arrived.wait_recv()
        parts, c, y, x = self.parts, self.c, self.y, self.x
        half = TILES // 2

        def add(t, carry):
            parts[c, y, k, t] = (
                parts[c, y, k, t].astype(jnp.float32) + self.from_y[k, t].astype(jnp.float32)
            ).astype(jnp.bfloat16)
            return carry

        lax.fori_loop(0, TILES, add, 0)
        return self.start(
            k, 2, parts.at[c, y, k, pl.ds((1 - x) * half, half)], self.from_x.at[k], self.x_partner
        )

    def stage_z(self, k, arrived):
        arrived.wait_recv()
        parts, c, y, x = self.parts, self.c, self.y, self.x
        half = TILES // 2

        def add(t, carry):
            parts[c, y, k, x * half + t] = (
                parts[c, y, k, x * half + t].astype(jnp.float32)
                + self.from_x[k, t].astype(jnp.float32)
            ).astype(jnp.bfloat16)
            return carry

        lax.fori_loop(0, half, add, 0)
        return [
            self.start(
                k,
                2 + d,
                parts.at[c, y, k, x * half + lax.rem(self.z + d, 4)],
                self.from_z.at[k, d - 1],
                self.z_partners[d - 1],
            )
            for d in range(1, 4)
        ]

    def stage_back(self, k, arrived):
        for copy in arrived:
            copy.wait_recv()
        final = self.final
        spot = self.x * (TILES // 2) + self.z
        total = self.parts[self.c, self.y, k, spot].astype(jnp.float32)
        for d in range(3):
            total = total + self.from_z[k, d].astype(jnp.float32)
        for step, partner in enumerate(self.far_partners):
            self.from_far[k, 2 * step] = total.astype(jnp.bfloat16)
            copy = self.start(
                k,
                9 + step,
                self.from_far.at[k, 2 * step],
                self.from_far.at[k, 2 * step + 1],
                partner,
            )
            copy.wait_recv()
            total = total + self.from_far[k, 2 * step + 1].astype(jnp.float32)
        final[k, spot] = total.astype(jnp.bfloat16)
        own = final.at[k, spot]
        return [self.start(k, 5 + d, own, own, self.z_partners[d - 1]) for d in range(1, 4)]

    def stage_back_x(self, k, arrived):
        for copy in arrived:
            copy.wait_recv()
        own = self.final.at[k, pl.ds(self.x * (TILES // 2), TILES // 2)]
        return self.start(k, 9 + len(self.far_partners), own, own, self.x_partner)

    def stage_end(self, k, arrived):
        arrived.wait_recv()


def reduction_scratch(replicas, chunks):
    far = max(replicas.bit_length() - 4, 0)
    tile = (144, 128)
    low = jnp.bfloat16
    return [
        pltpu.VMEM((2, 2, chunks, TILES) + tile, low),
        pltpu.VMEM((chunks, 2, TILES) + tile, low),
        pltpu.VMEM((chunks, TILES) + tile, low),
        pltpu.VMEM((chunks, TILES // 2) + tile, low),
        pltpu.VMEM((chunks, 3) + tile, low),
        pltpu.VMEM((chunks, 2 * max(far, 1)) + tile, low),
        pltpu.VMEM((chunks, TILES) + tile, low),
        pltpu.SemaphoreType.DMA((chunks, 10 + far)),
        pltpu.SemaphoreType.DMA((chunks, 10 + far)),
    ]


def put_columns(parts, chunk, tile, product):
    product = product.astype(jnp.bfloat16)
    for s in range(4):
        rows = product[144 * s : 144 * s + 144]
        for j in range(product.shape[1] // 128):
            parts[s % 2, s // 2, chunk, tile + j] = rows[:, j * 128 : j * 128 + 128]


def wide_dot(left, right):
    return jnp.dot(left, right, preferred_element_type=jnp.float32)


FEED_CHUNKS = 5


def feed_kernel(
    replicas,
    normed_two_t,
    attended_t,
    out_grad_t,
    grad_gate,
    grad_up,
    grad_branch,
    hidden,
    bias_t,
    window,
    queries_t,
    grad_attended_t,
    queries_rows,
    grad_attended_rows,
    log_total,
    delta,
    out_gate,
    out_up,
    out_down,
    out_branch,
    grad_window,
    grad_queries_t,
    *scratch,
):
    work = Reduction(replicas, FEED_CHUNKS, scratch[:7], scratch[7], scratch[8])
    parts, final = work.parts, work.final
    work.greet()

    def down_part(chunk, tile, j):
        for s in range(4):
            columns = slice(s * 384 + j * 128, s * 384 + j * 128 + 128)
            product = wide_dot(out_grad_t[...], hidden[:, columns]).astype(jnp.bfloat16)
            for row in range(4):
                parts[s % 2, s // 2, chunk, tile + row] = product[144 * row : 144 * row + 144]

    def columns_part(chunk, tile, left, right, first, last):
        for column in range(first, last, 256):
            put_columns(
                parts,
                chunk,
                tile + (column - first) // 128,
                wide_dot(left[...], right[:, column : column + 256]),
            )

    def products(k):
        if k == 0:
            columns_part(0, 0, normed_two_t, grad_gate, 0, 1024)
        elif k == 1:
            columns_part(1, 0, normed_two_t, grad_gate, 1024, 1536)
            columns_part(1, 4, normed_two_t, grad_up, 0, 512)
        elif k == 2:
            columns_part(2, 0, normed_two_t, grad_up, 512, 1536)
        elif k == 3:
            down_part(3, 0, 0)
            down_part(3, 4, 1)
        else:
            down_part(4, 0, 2)
            columns_part(4, 4, attended_t, grad_branch, 0, 512)

    def write_out(k):
        def columns(target, column, first, count):
            for t in range(count):
                target[:, column + t * 128 : column + t * 128 + 128] = final[k, first + t].astype(
                    jnp.float32
                )

        def rows(first, j):
            block = jnp.concatenate(
                [final[k, first + row].astype(jnp.float32) for row in range(4)], axis=0
            )
            out_down[j * 128 : j * 128 + 128, :] = block.T

        if k == 0:
            columns(out_gate, 0, 0, 8)
        elif k == 1:
            columns(out_gate, 1024, 0, 4)
            columns(out_up, 0, 4, 4)
        elif k == 2:
            columns(out_up, 512, 0, 8)
        elif k == 3:
            rows(0, 0)
            rows(4, 1)
        else:
            rows(0, 2)
            columns(out_branch, 0, 4, 4)

    def attend(c, third):
        lanes = slice(c * 128, c * 128 + 128)
        q_t = queries_t[c]
        a_t = grad_attended_t[c]

        def block(i, carry):
            slot = third * 3 + i
            kv = window[slot, :, lanes]
            bias = bias_t[slot]
            bias = jnp.concatenate([bias, bias, bias], axis=1)
            probs = jnp.exp(wide_dot(kv, q_t) + bias - log_total[c])
            grads = probs * (wide_dot(kv, a_t) - delta[c])
            grads = grads.astype(jnp.bfloat16)
            back = wide_dot(grads, queries_rows[c]) + wide_dot(
                probs.astype(jnp.bfloat16), grad_attended_rows[c]
            )
            grad_window[slot, :, lanes] = back.astype(jnp.bfloat16)
            return carry + contract_rows(kv, grads)

        start = jnp.zeros((128, 768), jnp.float32)
        done = lax.fori_loop(0, 3, block, start)
        if third == 0:
            grad_queries_t[c] = done[:64]
        else:
            grad_queries_t[c] += done[:64]

    last = len(work.stages) - 1
    for t in range(FEED_CHUNKS + last):
        for k in range(FEED_CHUNKS):
            stage = t - k
            if stage == 0:
                products(k)
            if 0 <= stage <= last:
                work.advance(k, stage)
            if stage == last:
                write_out(k)
        if t < 9:
            attend(t // 3, t % 3)
    work.finish()


def feed_and_attention_back(replicas, *operands):
    vmem = pl.BlockSpec(memory_space=pltpu.VMEM)
    wide = jnp.float32
    shapes = [
        jax.ShapeDtypeStruct((144, 1536), wide),
        jax.ShapeDtypeStruct((144, 1536), wide),
        jax.ShapeDtypeStruct((384, 576), wide),
        jax.ShapeDtypeStruct((144, 512), wide),
        jax.ShapeDtypeStruct((9, 256, 384), jnp.bfloat16),
        jax.ShapeDtypeStruct((3, 64, 768), wide),
    ]
    return pl.pallas_call(
        functools.partial(feed_kernel, replicas),
        out_shape=shapes,
        in_specs=[vmem] * len(operands),
        out_specs=[vmem] * len(shapes),
        scratch_shapes=reduction_scratch(replicas, FEED_CHUNKS),
        compiler_params=pltpu.CompilerParams(
            collective_id=4, has_side_effects=True, vmem_limit_bytes=VMEM_LIMIT
        ),
    )(*operands)


def tail_kernel(
    replicas,
    normed_one_t,
    attended_t,
    grad_cols,
    gains,
    out_cols,
    out_gains,
    *scratch,
):
    work = Reduction(replicas, 1, scratch[:7], scratch[7], scratch[8])
    tally, from_gain, gain_sends, gain_recvs = scratch[9:]
    work.greet()
    for pair in range(4):
        right = grad_cols[:, pair * 256 : pair * 256 + 256]
        product = wide_dot(normed_one_t[...], right)
        if pair == 3:
            lane = lax.broadcasted_iota(jnp.int32, product.shape, 1)
            product = jnp.where(lane < 192, product, wide_dot(attended_t[...], right))
        put_columns(work.parts, 0, 2 * pair, product)
    gain_steps = [[work.core_partner], [work.y_partner], [work.x_partner], work.z_partners]
    gain_steps += [[partner] for partner in work.far_partners]
    tally[0] = gains[...]
    flight = []
    slot = 0
    for t in range(max(len(work.stages), len(gain_steps) + 1)):
        if t < len(work.stages):
            work.advance(0, t)
        if flight:
            total = tally[t - 1]
            for copy, landed in flight:
                copy.wait_recv()
                total = total + from_gain[landed]
            flight = []
            if t < len(gain_steps):
                tally[t] = total
            else:
                out_gains[...] = total
        if t < len(gain_steps):
            for partner in gain_steps[t]:
                copy = remote(
                    tally.at[t], from_gain.at[slot], gain_sends.at[slot], gain_recvs.at[slot], partner
                )
                copy.start()
                work.pending.append(copy)
                flight.append((copy, slot))
                slot += 1
    for t in range(TILES):
        out_cols[:, t * 128 : t * 128 + 128] = work.final[0, t].astype(jnp.float32)
    work.finish()


def reduce_tail(replicas, *operands):
    vmem = pl.BlockSpec(memory_space=pltpu.VMEM)
    wide = jnp.float32
    far = max(replicas.bit_length() - 4, 0)
    return pl.pallas_call(
        functools.partial(tail_kernel, replicas),
        out_shape=[
            jax.ShapeDtypeStruct((144, 1024), wide),
            jax.ShapeDtypeStruct((8, 256), wide),
        ],
        in_specs=[vmem] * len(operands),
        out_specs=[vmem] * 2,
        scratch_shapes=reduction_scratch(replicas, 1)
        + [
            pltpu.VMEM((4 + far, 8, 256), wide),
            pltpu.VMEM((6 + far, 8, 256), wide),
            pltpu.SemaphoreType.DMA((6 + far,)),
            pltpu.SemaphoreType.DMA((6 + far,)),
        ],
        compiler_params=pltpu.CompilerParams(
            collective_id=5, has_side_effects=True, vmem_limit_bytes=VMEM_LIMIT
        ),
    )(*operands)


def per_device(
    inputs,
    seg_ids,
    seq_starts,
    gain_one,
    query_w,
    key_w,
    value_weight,
    out_w,
    gain_two,
    gate_w,
    up_w,
    down_w,
    out_grad,
):
    qkvo_all, gate_all, up_all, down_all = gather_weights(
        jnp.concatenate([query_w, key_w, value_weight, out_w], axis=1), gate_w, up_w, down_w
    )
    qkvo_all, gate_all, up_all, down_all = (
        a.reshape(a.shape[0] * a.shape[1], a.shape[2]) for a in (qkvo_all, gate_all, up_all, down_all)
    )
    joined_w = qkvo_all[:, : query_w.shape[1] + 2 * key_w.shape[1]]
    out_all = qkvo_all[:, query_w.shape[1] + 2 * key_w.shape[1] :]
    query_all = qkvo_all[:, : query_w.shape[1]]
    key_all = qkvo_all[:, query_w.shape[1] : query_w.shape[1] + key_w.shape[1]]
    gain_one_all = lax.all_gather(gain_one, "group", axis=0, tiled=True)
    gain_two_all = lax.all_gather(gain_two, "group", axis=0, tiled=True)
    tok_rows = inputs.shape[0]
    query_heads = query_all.shape[1] // HEAD_DIM
    kv_heads = key_all.shape[1] // HEAD_DIM
    repeat_heads = query_heads // kv_heads
    kv_width = kv_heads * HEAD_DIM
    score_scale = 1.0 / math.sqrt(HEAD_DIM)
    reach_back = SEQUENCE_LENGTH // tok_rows
    window_rows = (reach_back + 1) * tok_rows
    device = lax.axis_index(("replica", "group"))
    token_index = device * tok_rows + jnp.arange(tok_rows, dtype=jnp.int32)
    segment_table = jnp.arange(seq_starts.shape[0], dtype=jnp.int32)
    first_token = jnp.sum(
        jnp.where(seg_ids[:, None] == segment_table[None, :], seq_starts[None, :], 0), axis=1
    )
    rotary_angles = rope_angles(token_index - first_token, HEAD_DIM)
    key_index = (device - reach_back) * tok_rows + jnp.arange(window_rows, dtype=jnp.int32)
    visible = (key_index[None, :] <= token_index[:, None]) & (
        key_index[None, :] >= first_token[:, None]
    )
    inputs_wide = inputs.astype(jnp.float32)
    scale_one = rms_scale(inputs_wide)
    gain_one_wide = gain_one_all.astype(jnp.float32)
    first_normed = (inputs_wide * scale_one * gain_one_wide).astype(jnp.bfloat16)
    projected = jnp.dot(first_normed, joined_w, preferred_element_type=jnp.float32)
    query_cols = query_heads * HEAD_DIM
    queries = apply_rotary(
        projected[:, :query_cols].reshape(tok_rows, query_heads, HEAD_DIM), rotary_angles
    ).astype(jnp.bfloat16)
    key_matrix = apply_rotary(
        projected[:, query_cols : query_cols + kv_width].reshape(tok_rows, kv_heads, HEAD_DIM),
        rotary_angles,
    )
    value_matrix = projected[:, query_cols + kv_width :].astype(jnp.bfloat16)
    packed = jnp.concatenate(
        [
            key_matrix.astype(jnp.bfloat16),
            value_matrix.reshape(tok_rows, kv_heads, HEAD_DIM),
        ],
        axis=2,
    ).reshape(tok_rows, 2 * kv_width)
    window_blocks = exchange_window(packed)
    window = window_blocks.reshape(window_rows, kv_heads, 2 * HEAD_DIM)
    key_grid = window[:, :, :HEAD_DIM]
    value_grid = window[:, :, HEAD_DIM:]
    query_grid = queries.reshape(tok_rows, kv_heads, repeat_heads, HEAD_DIM)

    def masked_scores():
        raw_scores = (
            jnp.einsum("tcrd,wcd->crtw", query_grid, key_grid, preferred_element_type=jnp.float32)
            * score_scale
        )
        return jnp.where(visible, raw_scores, masked_score)

    scores = masked_scores()
    row_peak = jnp.max(scores, axis=-1, keepdims=True)
    exponent = jnp.exp(scores - row_peak)
    row_total = jnp.sum(exponent, axis=-1, keepdims=True)
    log_total = row_peak + jnp.log(row_total)
    probs_low = (exponent / row_total).astype(jnp.bfloat16)
    attended_wide = jnp.einsum(
        "crtw,wcd->tcrd", probs_low, value_grid, preferred_element_type=jnp.float32
    )
    attended = attended_wide.reshape(tok_rows, query_cols).astype(jnp.bfloat16)
    middle = inputs_wide + jnp.dot(attended, out_all, preferred_element_type=jnp.float32)
    scale_two = rms_scale(middle)
    gain_two_wide = gain_two_all.astype(jnp.float32)
    normed_two = (middle * scale_two * gain_two_wide).astype(jnp.bfloat16)
    gate = jnp.dot(normed_two, gate_all, preferred_element_type=jnp.float32)
    upper = jnp.dot(normed_two, up_all, preferred_element_type=jnp.float32)
    sigmoid_gate = jax.nn.sigmoid(gate)
    hidden = (gate * sigmoid_gate * upper).astype(jnp.bfloat16)
    outputs = middle + jnp.dot(hidden, down_all, preferred_element_type=jnp.float32)
    grad_hidden = times_transpose(out_grad, down_all)
    grad_gate = (grad_hidden * upper * sigmoid_gate * (1.0 + gate * (1.0 - sigmoid_gate))).astype(
        jnp.bfloat16
    )
    grad_up = (grad_hidden * gate * sigmoid_gate).astype(jnp.bfloat16)
    grad_normed_two = times_transpose(grad_gate, gate_all) + times_transpose(grad_up, up_all)
    grad_middle_norm, grad_gain_two = norm_back(grad_normed_two, middle, scale_two, gain_two_wide)
    grad_middle = out_grad.astype(jnp.float32) + grad_middle_norm
    grad_branch = grad_middle.astype(jnp.bfloat16)
    grad_attended = (
        times_transpose(grad_branch, out_all)
        .astype(jnp.bfloat16)
        .reshape(tok_rows, kv_heads, repeat_heads, HEAD_DIM)
    )
    delta = jnp.sum(grad_attended.astype(jnp.float32) * attended_wide, axis=-1)
    delta = delta.transpose(1, 2, 0).reshape(kv_heads, 1, repeat_heads * tok_rows)
    bias = jnp.where(
        (key_index[:, None] <= token_index[None, :]) & (key_index[:, None] >= first_token[None, :]),
        0.0,
        masked_score,
    ).reshape(reach_back + 1, tok_rows, tok_rows)
    query_rows = (query_grid * jnp.bfloat16(score_scale)).transpose(1, 2, 0, 3)
    query_rows = query_rows.reshape(kv_heads, repeat_heads * tok_rows, HEAD_DIM)
    attended_rows = grad_attended.transpose(1, 2, 0, 3)
    attended_rows = attended_rows.reshape(kv_heads, repeat_heads * tok_rows, HEAD_DIM)
    query_rows = jnp.pad(query_rows, ((0, 0), (0, 0), (0, HEAD_DIM)))
    attended_rows = jnp.pad(attended_rows, ((0, 0), (0, 0), (HEAD_DIM, 0)))
    attended_t = attended.T
    out_gate, out_up, grad_down_w, out_branch, grad_window, grad_query_t = feed_and_attention_back(
        lax.axis_size("replica"),
        normed_two.T,
        attended_t,
        out_grad.T,
        grad_gate,
        grad_up,
        grad_branch,
        hidden,
        bias,
        window_blocks,
        query_rows.transpose(0, 2, 1),
        attended_rows.transpose(0, 2, 1),
        query_rows,
        attended_rows,
        log_total.reshape(kv_heads, 1, repeat_heads * tok_rows),
        delta,
    )
    grad_query_rot = (
        grad_query_t.reshape(kv_heads, HEAD_DIM, repeat_heads, tok_rows).transpose(3, 0, 2, 1)
        * score_scale
    )
    own_grad = return_window(grad_window).reshape(tok_rows, kv_heads, 2 * HEAD_DIM)
    grad_keys = apply_rotary(own_grad[:, :, :HEAD_DIM], -rotary_angles)
    grad_keys = grad_keys.reshape(tok_rows, kv_width).astype(jnp.bfloat16)
    grad_values = own_grad[:, :, HEAD_DIM:].reshape(tok_rows, kv_width).astype(jnp.bfloat16)
    grad_queries = apply_rotary(
        grad_query_rot.reshape(tok_rows, query_heads, HEAD_DIM), -rotary_angles
    )
    grad_queries = grad_queries.reshape(tok_rows, query_cols).astype(jnp.bfloat16)
    grad_qkv = jnp.concatenate([grad_queries, grad_keys, grad_values], axis=1)
    grad_normed_one = times_transpose(grad_qkv, joined_w)
    grad_inputs_norm, grad_gain_one = norm_back(
        grad_normed_one, inputs_wide, scale_one, gain_one_wide
    )
    grad_inputs = grad_middle + grad_inputs_norm
    width = gain_one_all.shape[0]
    gain_grads = jnp.pad(jnp.concatenate([grad_gain_one, grad_gain_two]), (0, 2048 - 2 * width))
    tail, gain_sums = reduce_tail(
        lax.axis_size("replica"),
        first_normed.T,
        attended_t,
        jnp.concatenate([grad_qkv, grad_branch[:, 512:]], axis=1),
        gain_grads.reshape(8, 256),
    )
    gain_sums = gain_sums.reshape(2048)[: 2 * width].reshape(2, width)
    shard = width // lax.axis_size("group")
    gain_sums = lax.dynamic_slice_in_dim(gain_sums, lax.axis_index("group") * shard, shard, 1)
    first = query_cols
    second = first + kv_width
    third = second + kv_width
    return (
        outputs,
        grad_inputs,
        gain_sums[0],
        tail[:, :first],
        tail[:, first:second],
        tail[:, second:third],
        jnp.concatenate([out_branch, tail[:, third:]], axis=1),
        gain_sums[1],
        out_gate,
        out_up,
        grad_down_w,
    )


def solution(mesh):
    placed = (
        P(("replica", "group"), None),
        P(("replica", "group")),
        P(),
        P("group"),
        P("group", None),
        P("group", None),
        P("group", None),
        P("group", None),
        P("group"),
        P("group", None),
        P("group", None),
        P("group", None),
        P(("replica", "group"), None),
    )
    return jax.shard_map(
        per_device,
        mesh=mesh,
        in_specs=placed,
        out_specs=(
            P(("replica", "group"), None),
            P(("replica", "group"), None),
            P("group"),
            P("group", None),
            P("group", None),
            P("group", None),
            P("group", None),
            P("group"),
            P("group", None),
            P("group", None),
            P("group", None),
        ),
        check_vma=False,
    )
```

```python
import functools
import math

import jax
import jax.numpy as jnp
from jax import lax
from jax.experimental import pallas as pl
from jax.experimental.pallas import tpu as pltpu
from jax.sharding import PartitionSpec as P

HEAD_DIM = 64
SEQUENCE_LENGTH = 2048


epsilon = 1e-05
rope_base = 100000.0
masked_score = -1e30


def from_behind(block, axis, distance):
    devices = range(lax.axis_size(axis))
    route = [(i - distance, i) for i in devices if i - distance in devices]
    return lax.ppermute(block, axis, route)


def rms_scale(value_matrix):
    return lax.rsqrt(jnp.mean(value_matrix * value_matrix, axis=-1, keepdims=True) + epsilon)


def rope_angles(positions, head_size):
    frequency = jnp.exp(
        jnp.arange(0, head_size, 2, dtype=jnp.float32) * (-math.log(rope_base) / head_size)
    )
    return positions.astype(jnp.float32)[:, None] * frequency[None, :]


def apply_rotary(value_matrix, rotary_angles):
    middle_cut = value_matrix.shape[-1] // 2
    former = value_matrix[..., :middle_cut]
    latter = value_matrix[..., middle_cut:]
    cosine = jnp.cos(rotary_angles)[:, None, :]
    sine_part = jnp.sin(rotary_angles)[:, None, :]
    return jnp.concatenate(
        [former * cosine - latter * sine_part, latter * cosine + former * sine_part], axis=-1
    )


def contract_rows(former, latter):
    return lax.dot_general(
        former, latter, (((0,), (0,)), ((), ())), preferred_element_type=jnp.float32
    )


def times_transpose(former, latter):
    return lax.dot_general(
        former, latter, (((1,), (1,)), ((), ())), preferred_element_type=jnp.float32
    )


def norm_back(grad_normed, value_matrix, scale_rows, gain_wide):
    weighted = grad_normed * gain_wide
    cubed = scale_rows * scale_rows * scale_rows
    grad_values = scale_rows * weighted - value_matrix * cubed * jnp.mean(
        weighted * value_matrix, axis=-1, keepdims=True
    )
    grad_gain = jnp.sum(grad_normed * value_matrix * scale_rows, axis=0)
    return (grad_values, grad_gain)


MESH = pl.DeviceIdType.MESH
VMEM_LIMIT = 56 * 1024 * 1024


def flip_bit(index, bit):
    return index + bit - 2 * bit * (lax.rem(lax.div(index, bit), 2))


def greet(partners):
    barrier = pltpu.get_barrier_semaphore()
    for partner in partners:
        pl.semaphore_signal(barrier, inc=1, device_id=partner, device_id_type=MESH)
    pl.semaphore_wait(barrier, len(partners))


def remote(source, target, send_sem, recv_sem, partner):
    return pltpu.make_async_remote_copy(
        src_ref=source,
        dst_ref=target,
        send_sem=send_sem,
        recv_sem=recv_sem,
        device_id=partner,
        device_id_type=MESH,
    )


def half_of(shard, part):
    if shard.shape[-1] % 256 == 0:
        width = shard.shape[-1] // 2
        return shard.at[:, pl.ds(pl.multiple_of(part * width, 128), width)]
    height = shard.shape[-2] // 2
    return shard.at[pl.ds(pl.multiple_of(part * height, 16), height), :]


class Gather:
    def __init__(self, shards, wholes, sends, recvs, local):
        self.shards, self.wholes = shards, wholes
        self.sends, self.recvs, self.local = sends, recvs, local
        r = lax.axis_index("replica")
        self.g = lax.axis_index("group")
        self.x = lax.rem(r, 2)
        self.core_partner = (r, flip_bit(self.g, 1))
        self.y_partner = (r, flip_bit(self.g, 2))
        self.x_partner = (flip_bit(r, 1), self.g)
        self.across = flip_bit(self.g, 2)
        self.from_y, self.from_x, self.full, self.own = [], [], [], []

    def start(self, i, slot, source, target, partner):
        copy = remote(source, target, self.sends.at[i, slot], self.recvs.at[i, slot], partner)
        copy.start()
        return copy

    def begin(self):
        for i, (shard, whole) in enumerate(zip(self.shards, self.wholes)):
            self.from_y.append(
                self.start(
                    i,
                    0,
                    half_of(shard, self.x),
                    half_of(whole.at[self.g], self.x),
                    self.y_partner,
                )
            )
        for i, (shard, whole) in enumerate(zip(self.shards, self.wholes)):
            self.full.append(self.start(i, 1, shard, whole.at[self.g], self.core_partner))
            own = pltpu.make_async_copy(shard, whole.at[self.g], self.local.at[i])
            own.start()
            self.own.append(own)

    def pass_y(self):
        for i, whole in enumerate(self.wholes):
            self.from_y[i].wait_recv()
            piece = half_of(whole.at[self.across], self.x)
            self.from_x.append(self.start(i, 2, piece, piece, self.x_partner))
            self.full.append(self.start(i, 3, piece, piece, self.core_partner))

    def pass_x(self):
        for i, whole in enumerate(self.wholes):
            self.from_x[i].wait_recv()
            piece = half_of(whole.at[self.across], 1 - self.x)
            self.full.append(self.start(i, 4, piece, piece, self.core_partner))

    def finish(self):
        for copy in self.own + self.full:
            copy.wait()
        for copy in self.from_y + self.from_x:
            copy.wait_send()


def gather_kernel(count, *refs):
    work = Gather(refs[:count], refs[count : 2 * count], *refs[2 * count :])
    greet((work.core_partner, work.y_partner, work.x_partner))
    work.begin()
    work.pass_y()
    work.pass_x()
    work.finish()


def gather_scratch(count):
    return [
        pltpu.SemaphoreType.DMA((count, 5)),
        pltpu.SemaphoreType.DMA((count, 5)),
        pltpu.SemaphoreType.DMA((count,)),
    ]


def gather_weights(*arrays):
    vmem = pl.BlockSpec(memory_space=pltpu.VMEM)
    return pl.pallas_call(
        functools.partial(gather_kernel, len(arrays)),
        out_shape=[jax.ShapeDtypeStruct((4,) + a.shape, a.dtype) for a in arrays],
        in_specs=[vmem] * len(arrays),
        out_specs=[vmem] * len(arrays),
        scratch_shapes=gather_scratch(len(arrays)),
        compiler_params=pltpu.CompilerParams(
            collective_id=1, has_side_effects=True, vmem_limit_bytes=VMEM_LIMIT
        ),
    )(*arrays)


def place():
    r = lax.axis_index("replica")
    g = lax.axis_index("group")
    slabs = lax.axis_size("replica") // 2
    slab = lax.div(r, 2)
    return r, g, slabs, slab


def slot_of(block, here):
    return lax.rem(block - here + 8, 8)


def forward_kernel(
    packed,
    gate,
    up,
    down,
    queries_t,
    bias_t,
    window,
    gate_all,
    up_all,
    down_all,
    attended_t,
    log_total,
    peak,
    sums,
    mixed,
    sends,
    recvs,
    local,
    *gather_refs,
):
    r, g, slabs, slab = place()
    x = lax.rem(r, 2)
    y = lax.div(g, 2)
    c = lax.rem(g, 2)
    rx, gy, gc = flip_bit(r, 1), flip_bit(g, 2), flip_bit(g, 1)
    here = x * 4 + g
    at_x, at_y, at_c = (1 - x) * 4 + g, x * 4 + gy, x * 4 + gc
    at_xy = (1 - x) * 4 + gy
    far_x, far_y = (1 - x) * 4 + gc, x * 4 + flip_bit(gc, 2)
    far_xy = (1 - x) * 4 + flip_bit(gc, 2)
    ahead = (2 * lax.rem(slab + 1, slabs) + x, g)
    behind = (2 * lax.rem(slab + slabs - 1, slabs) + x, g)
    barrier = pltpu.get_barrier_semaphore()
    for partner in ((rx, g), (r, gy), (r, gc), behind):
        pl.semaphore_signal(barrier, inc=1, device_id=partner, device_id_type=MESH)
    pl.semaphore_wait(barrier, 4)
    weights = Gather((gate, up, down), (gate_all, up_all, down_all), *gather_refs)
    to_ahead = remote(packed, window.at[0], sends.at[0], recvs.at[0], ahead)
    to_ahead.start()
    firsts = []
    for i, (bit, partner, there) in enumerate(
        ((x, (rx, g), at_x), (y, (r, gy), at_y), (c, (r, gc), at_c))
    ):
        target = window.at[slot_of(here, there)]
        early = remote(packed, target, sends.at[1 + i], recvs.at[1 + i], partner)
        late = remote(window.at[0], target, sends.at[1 + i], recvs.at[1 + i], partner)
        firsts.append((bit, early, late))
    for bit, early, late in firsts:
        pl.when(bit == 0)(early.start)
    own = pltpu.make_async_copy(packed, window.at[8], local)
    own.start()
    weights.begin()

    def attend(slot, first=False):
        for head in range(3):
            kv = window[slot, :, head * 128 : head * 128 + 128]
            bias = bias_t[slot]
            scores = wide_dot(kv, queries_t[head]) + jnp.concatenate([bias, bias, bias], axis=1)
            top = jnp.max(scores, axis=0, keepdims=True)
            if not first:
                before = peak[head]
                top = jnp.maximum(before, top)
                fade = jnp.exp(before - top)
            exponent = jnp.exp(scores - top)
            part = jnp.sum(exponent, axis=0, keepdims=True)
            block = contract_rows(kv, exponent.astype(jnp.bfloat16))
            peak[head] = top
            if first:
                sums[head] = part
                mixed[head] = block
            else:
                sums[head] = sums[head] * fade + part
                mixed[head] = mixed[head] * fade + block

    own.wait()
    attend(8, True)
    to_ahead.wait_recv()
    for bit, early, late in firsts:
        pl.when(bit == 1)(late.start)
    attend(0)
    firsts[0][1].wait_recv()
    slot_x = window.at[slot_of(at_x, here)]
    diagonal = remote(
        slot_x, window.at[slot_of(at_x, at_y)], sends.at[4], recvs.at[4], (r, gy)
    )
    diagonal.start()
    core_x = remote(slot_x, window.at[slot_of(at_x, at_c)], sends.at[5], recvs.at[5], (r, gc))
    core_x.start()
    firsts[1][1].wait_recv()
    slot_y = window.at[slot_of(at_y, here)]
    core_y = remote(slot_y, window.at[slot_of(at_y, at_c)], sends.at[6], recvs.at[6], (r, gc))
    core_y.start()
    attend(slot_of(at_x, here))
    weights.pass_y()
    attend(slot_of(at_y, here))
    diagonal.wait_recv()
    slot_xy = window.at[slot_of(at_xy, here)]
    core_xy = remote(slot_xy, window.at[slot_of(at_xy, at_c)], sends.at[7], recvs.at[7], (r, gc))
    core_xy.start()
    attend(slot_of(at_xy, here))
    firsts[2][1].wait_recv()
    attend(slot_of(at_c, here))
    core_x.wait_recv()
    attend(slot_of(far_x, here))
    weights.pass_x()
    core_y.wait_recv()
    attend(slot_of(far_y, here))
    core_xy.wait_recv()
    attend(slot_of(far_xy, here))
    for head in range(3):
        out = mixed[head][64:] / sums[head]
        for row in range(3):
            spot = (head * 3 + row) * 64
            attended_t[spot : spot + 64, :] = out[:, row * 256 : row * 256 + 256]
        log_total[head] = peak[head] + jnp.log(sums[head])
    weights.finish()
    for copy in (to_ahead, firsts[0][1], firsts[1][1], firsts[2][1], diagonal, core_x, core_y, core_xy):
        copy.wait_send()


def forward_attention(packed, gate, up, down, queries_t, bias_t):
    vmem = pl.BlockSpec(memory_space=pltpu.VMEM)
    wide = jnp.float32
    shapes = [jax.ShapeDtypeStruct((9,) + packed.shape, packed.dtype)]
    shapes += [jax.ShapeDtypeStruct((4,) + a.shape, a.dtype) for a in (gate, up, down)]
    shapes += [
        jax.ShapeDtypeStruct((576, 256), wide),
        jax.ShapeDtypeStruct((3, 1, 768), wide),
    ]
    return pl.pallas_call(
        forward_kernel,
        out_shape=shapes,
        in_specs=[vmem] * 6,
        out_specs=[vmem] * len(shapes),
        scratch_shapes=[
            pltpu.VMEM((3, 1, 768), wide),
            pltpu.VMEM((3, 1, 768), wide),
            pltpu.VMEM((3, 128, 768), wide),
            pltpu.SemaphoreType.DMA((8,)),
            pltpu.SemaphoreType.DMA((8,)),
            pltpu.SemaphoreType.DMA,
        ]
        + gather_scratch(3),
        compiler_params=pltpu.CompilerParams(
            collective_id=2, has_side_effects=True, vmem_limit_bytes=VMEM_LIMIT
        ),
    )(packed, gate, up, down, queries_t, bias_t)


def return_kernel(window, total, outgoing, landed, sums, sends, recvs):
    r, g, slabs, slab = place()
    x = lax.rem(r, 2)
    y = lax.div(g, 2)
    c = lax.rem(g, 2)
    rx, gy, gc = flip_bit(r, 1), flip_bit(g, 2), flip_bit(g, 1)
    here = x * 4 + g
    at_x, at_y, at_c = (1 - x) * 4 + g, x * 4 + gy, x * 4 + gc
    at_xy = (1 - x) * 4 + gy
    far = [x * 4 + gc, x * 4 + flip_bit(gc, 2), (1 - x) * 4 + gc, (1 - x) * 4 + flip_bit(gc, 2)]
    ahead = (2 * lax.rem(slab + 1, slabs) + x, g)
    behind = (2 * lax.rem(slab + slabs - 1, slabs) + x, g)
    barrier = pltpu.get_barrier_semaphore()
    for partner in ((rx, g), (r, gy), (r, gc), ahead):
        pl.semaphore_signal(barrier, inc=1, device_id=partner, device_id_type=MESH)
    pl.semaphore_wait(barrier, 4)
    wide = jnp.float32
    low = jnp.bfloat16
    core = []
    for i in (3, 1, 2, 0):
        copy = remote(
            window.at[slot_of(far[i], here)], landed.at[i], sends.at[i], recvs.at[i], (r, gc)
        )
        copy.start()
        core.append(copy)

    def blend(bit, index):
        block = landed[index].astype(wide)
        zero = jnp.zeros_like(block)
        total[...] += jnp.where(bit == 0, block, zero)
        sums[...] += jnp.where(bit == 1, block, zero)

    core[0].wait_recv()
    outgoing[0] = (window[slot_of(at_xy, here)].astype(wide) + landed[3].astype(wide)).astype(low)
    to_y_diagonal = remote(outgoing.at[0], landed.at[4], sends.at[4], recvs.at[4], (r, gy))
    to_y_diagonal.start()
    core[1].wait_recv()
    outgoing[1] = (window[slot_of(at_y, here)].astype(wide) + landed[1].astype(wide)).astype(low)
    to_y = remote(outgoing.at[1], landed.at[5], sends.at[5], recvs.at[5], (r, gy))
    to_y.start()
    core[2].wait_recv()
    to_y_diagonal.wait_recv()
    outgoing[2] = (
        window[slot_of(at_x, here)].astype(wide) + landed[2].astype(wide) + landed[4].astype(wide)
    ).astype(low)
    to_x = remote(outgoing.at[2], landed.at[6], sends.at[6], recvs.at[6], (rx, g))
    to_x.start()
    total[...] = window[8].astype(wide)
    sums[...] = window[0].astype(wide)
    core[3].wait_recv()
    blend(c, 0)
    to_y.wait_recv()
    blend(y, 5)
    to_x.wait_recv()
    blend(x, 6)
    outgoing[3] = sums[...].astype(low)
    to_behind = remote(outgoing.at[3], landed.at[7], sends.at[7], recvs.at[7], behind)
    to_behind.start()
    to_behind.wait_recv()
    total[...] += landed[7].astype(wide)
    for copy in core + [to_y_diagonal, to_y, to_x, to_behind]:
        copy.wait_send()


def return_window(window):
    block = window.shape[1:]
    vmem = pl.BlockSpec(memory_space=pltpu.VMEM)
    return pl.pallas_call(
        return_kernel,
        out_shape=jax.ShapeDtypeStruct(block, jnp.float32),
        in_specs=[vmem],
        out_specs=vmem,
        scratch_shapes=[
            pltpu.VMEM((4,) + block, window.dtype),
            pltpu.VMEM((8,) + block, window.dtype),
            pltpu.VMEM(block, jnp.float32),
            pltpu.SemaphoreType.DMA((8,)),
            pltpu.SemaphoreType.DMA((8,)),
        ],
        compiler_params=pltpu.CompilerParams(
            collective_id=3, has_side_effects=True, vmem_limit_bytes=VMEM_LIMIT
        ),
    )(window)


TILES = 8


class Reduction:
    def __init__(self, replicas, chunks, buffers, sends, recvs):
        (
            self.parts,
            self.from_core,
            self.from_y,
            self.from_x,
            self.from_z,
            self.from_far,
            self.final,
        ) = buffers
        self.sends, self.recvs = sends, recvs
        r = lax.axis_index("replica")
        g = lax.axis_index("group")
        self.c, self.y, self.x = lax.rem(g, 2), lax.div(g, 2), lax.rem(r, 2)
        self.z = lax.rem(lax.div(r, 2), 4)
        base = r - 2 * self.z
        self.core_partner = (r, flip_bit(g, 1))
        self.y_partner = (r, flip_bit(g, 2))
        self.x_partner = (flip_bit(r, 1), g)
        self.z_partners = [(base + 2 * lax.rem(self.z + d, 4), g) for d in (1, 2, 3)]
        self.far_partners = []
        bit = 8
        while bit < replicas:
            self.far_partners.append((flip_bit(r, bit), g))
            bit *= 2
        self.pending = []
        self.stages = (
            self.stage_core,
            self.stage_y,
            self.stage_x,
            self.stage_z,
            self.stage_back,
            self.stage_back_x,
            self.stage_end,
        )
        self.state = [None] * chunks

    def greet(self):
        greet(
            [self.core_partner, self.y_partner, self.x_partner] + self.z_partners + self.far_partners
        )

    def advance(self, chunk, stage):
        self.state[chunk] = self.stages[stage](chunk, self.state[chunk])

    def start(self, chunk, slot, source, target, partner):
        copy = remote(source, target, self.sends.at[chunk, slot], self.recvs.at[chunk, slot], partner)
        copy.start()
        self.pending.append(copy)
        return copy

    def finish(self):
        for copy in self.pending:
            copy.wait_send()

    def stage_core(self, k, arrived):
        return self.start(
            k, 0, self.parts.at[1 - self.c, :, k], self.from_core.at[k], self.core_partner
        )

    def stage_y(self, k, arrived):
        arrived.wait_recv()
        parts, c = self.parts, self.c

        def add(t, carry):
            for yy in range(2):
                parts[c, yy, k, t] = (
                    parts[c, yy, k, t].astype(jnp.float32)
                    + self.from_core[k, yy, t].astype(jnp.float32)
                ).astype(jnp.bfloat16)
            return carry

        lax.fori_loop(0, TILES, add, 0)
        return self.start(k, 1, parts.at[c, 1 - self.y, k], self.from_y.at[k], self.y_partner)

    def stage_x(self, k, arrived):
        arrived.wait_recv()
        parts, c, y, x = self.parts, self.c, self.y, self.x
        half = TILES // 2

        def add(t, carry):
            parts[c, y, k, t] = (
                parts[c, y, k, t].astype(jnp.float32) + self.from_y[k, t].astype(jnp.float32)
            ).astype(jnp.bfloat16)
            return carry

        lax.fori_loop(0, TILES, add, 0)
        return self.start(
            k, 2, parts.at[c, y, k, pl.ds((1 - x) * half, half)], self.from_x.at[k], self.x_partner
        )

    def stage_z(self, k, arrived):
        arrived.wait_recv()
        parts, c, y, x = self.parts, self.c, self.y, self.x
        half = TILES // 2

        def add(t, carry):
            parts[c, y, k, x * half + t] = (
                parts[c, y, k, x * half + t].astype(jnp.float32)
                + self.from_x[k, t].astype(jnp.float32)
            ).astype(jnp.bfloat16)
            return carry

        lax.fori_loop(0, half, add, 0)
        return [
            self.start(
                k,
                2 + d,
                parts.at[c, y, k, x * half + lax.rem(self.z + d, 4)],
                self.from_z.at[k, d - 1],
                self.z_partners[d - 1],
            )
            for d in range(1, 4)
        ]

    def stage_back(self, k, arrived):
        for copy in arrived:
            copy.wait_recv()
        final = self.final
        spot = self.x * (TILES // 2) + self.z
        total = self.parts[self.c, self.y, k, spot].astype(jnp.float32)
        for d in range(3):
            total = total + self.from_z[k, d].astype(jnp.float32)
        for step, partner in enumerate(self.far_partners):
            self.from_far[k, 2 * step] = total.astype(jnp.bfloat16)
            copy = self.start(
                k,
                9 + step,
                self.from_far.at[k, 2 * step],
                self.from_far.at[k, 2 * step + 1],
                partner,
            )
            copy.wait_recv()
            total = total + self.from_far[k, 2 * step + 1].astype(jnp.float32)
        final[k, spot] = total.astype(jnp.bfloat16)
        own = final.at[k, spot]
        return [self.start(k, 5 + d, own, own, self.z_partners[d - 1]) for d in range(1, 4)]

    def stage_back_x(self, k, arrived):
        for copy in arrived:
            copy.wait_recv()
        own = self.final.at[k, pl.ds(self.x * (TILES // 2), TILES // 2)]
        return self.start(k, 9 + len(self.far_partners), own, own, self.x_partner)

    def stage_end(self, k, arrived):
        arrived.wait_recv()


def reduction_scratch(replicas, chunks):
    far = max(replicas.bit_length() - 4, 0)
    tile = (144, 128)
    low = jnp.bfloat16
    return [
        pltpu.VMEM((2, 2, chunks, TILES) + tile, low),
        pltpu.VMEM((chunks, 2, TILES) + tile, low),
        pltpu.VMEM((chunks, TILES) + tile, low),
        pltpu.VMEM((chunks, TILES // 2) + tile, low),
        pltpu.VMEM((chunks, 3) + tile, low),
        pltpu.VMEM((chunks, 2 * max(far, 1)) + tile, low),
        pltpu.VMEM((chunks, TILES) + tile, low),
        pltpu.SemaphoreType.DMA((chunks, 10 + far)),
        pltpu.SemaphoreType.DMA((chunks, 10 + far)),
    ]


def put_columns(parts, chunk, tile, product):
    product = product.astype(jnp.bfloat16)
    for s in range(4):
        rows = product[144 * s : 144 * s + 144]
        for j in range(product.shape[1] // 128):
            parts[s % 2, s // 2, chunk, tile + j] = rows[:, j * 128 : j * 128 + 128]


def wide_dot(left, right):
    return jnp.dot(left, right, preferred_element_type=jnp.float32)


FEED_CHUNKS = 5


def feed_kernel(
    replicas,
    normed_two_t,
    attended_t,
    out_grad_t,
    grad_gate,
    grad_up,
    grad_branch,
    hidden,
    bias_t,
    window,
    queries_t,
    grad_attended_t,
    queries_rows,
    grad_attended_rows,
    log_total,
    delta,
    out_gate,
    out_up,
    out_down,
    out_branch,
    grad_window,
    grad_queries_t,
    *scratch,
):
    work = Reduction(replicas, FEED_CHUNKS, scratch[:7], scratch[7], scratch[8])
    parts, final = work.parts, work.final
    work.greet()

    def down_part(chunk, tile, j):
        for s in range(4):
            columns = slice(s * 384 + j * 128, s * 384 + j * 128 + 128)
            product = wide_dot(out_grad_t[...], hidden[:, columns]).astype(jnp.bfloat16)
            for row in range(4):
                parts[s % 2, s // 2, chunk, tile + row] = product[144 * row : 144 * row + 144]

    def columns_part(chunk, tile, left, right, first, last):
        for column in range(first, last, 256):
            put_columns(
                parts,
                chunk,
                tile + (column - first) // 128,
                wide_dot(left[...], right[:, column : column + 256]),
            )

    def products(k):
        if k == 0:
            columns_part(0, 0, normed_two_t, grad_gate, 0, 1024)
        elif k == 1:
            columns_part(1, 0, normed_two_t, grad_gate, 1024, 1536)
            columns_part(1, 4, normed_two_t, grad_up, 0, 512)
        elif k == 2:
            columns_part(2, 0, normed_two_t, grad_up, 512, 1536)
        elif k == 3:
            down_part(3, 0, 0)
            down_part(3, 4, 1)
        else:
            down_part(4, 0, 2)
            columns_part(4, 4, attended_t, grad_branch, 0, 512)

    def write_out(k):
        def columns(target, column, first, count):
            for t in range(count):
                target[:, column + t * 128 : column + t * 128 + 128] = final[k, first + t].astype(
                    jnp.float32
                )

        def rows(first, j):
            block = jnp.concatenate(
                [final[k, first + row].astype(jnp.float32) for row in range(4)], axis=0
            )
            out_down[j * 128 : j * 128 + 128, :] = block.T

        if k == 0:
            columns(out_gate, 0, 0, 8)
        elif k == 1:
            columns(out_gate, 1024, 0, 4)
            columns(out_up, 0, 4, 4)
        elif k == 2:
            columns(out_up, 512, 0, 8)
        elif k == 3:
            rows(0, 0)
            rows(4, 1)
        else:
            rows(0, 2)
            columns(out_branch, 0, 4, 4)

    def attend(c, third):
        lanes = slice(c * 128, c * 128 + 128)
        q_t = queries_t[c]
        a_t = grad_attended_t[c]

        def block(i, carry):
            slot = third * 3 + i
            kv = window[slot, :, lanes]
            bias = bias_t[slot]
            bias = jnp.concatenate([bias, bias, bias], axis=1)
            probs = jnp.exp(wide_dot(kv, q_t) + bias - log_total[c])
            grads = probs * (wide_dot(kv, a_t) - delta[c])
            grads = grads.astype(jnp.bfloat16)
            back = wide_dot(grads, queries_rows[c]) + wide_dot(
                probs.astype(jnp.bfloat16), grad_attended_rows[c]
            )
            grad_window[slot, :, lanes] = back.astype(jnp.bfloat16)
            return carry + contract_rows(kv, grads)

        start = jnp.zeros((128, 768), jnp.float32)
        done = lax.fori_loop(0, 3, block, start)
        if third == 0:
            grad_queries_t[c] = done[:64]
        else:
            grad_queries_t[c] += done[:64]

    last = len(work.stages) - 1
    for t in range(FEED_CHUNKS + last):
        for k in range(FEED_CHUNKS):
            stage = t - k
            if stage == 0:
                products(k)
            if 0 <= stage <= last:
                work.advance(k, stage)
            if stage == last:
                write_out(k)
        if t < 9:
            attend(t // 3, t % 3)
    work.finish()


def feed_and_attention_back(replicas, *operands):
    vmem = pl.BlockSpec(memory_space=pltpu.VMEM)
    wide = jnp.float32
    shapes = [
        jax.ShapeDtypeStruct((144, 1536), wide),
        jax.ShapeDtypeStruct((144, 1536), wide),
        jax.ShapeDtypeStruct((384, 576), wide),
        jax.ShapeDtypeStruct((144, 512), wide),
        jax.ShapeDtypeStruct((9, 256, 384), jnp.bfloat16),
        jax.ShapeDtypeStruct((3, 64, 768), wide),
    ]
    return pl.pallas_call(
        functools.partial(feed_kernel, replicas),
        out_shape=shapes,
        in_specs=[vmem] * len(operands),
        out_specs=[vmem] * len(shapes),
        scratch_shapes=reduction_scratch(replicas, FEED_CHUNKS),
        compiler_params=pltpu.CompilerParams(
            collective_id=4, has_side_effects=True, vmem_limit_bytes=VMEM_LIMIT
        ),
    )(*operands)


def tail_kernel(
    replicas,
    normed_one_t,
    attended_t,
    grad_cols,
    gains,
    out_cols,
    out_gains,
    *scratch,
):
    work = Reduction(replicas, 1, scratch[:7], scratch[7], scratch[8])
    tally, from_gain, gain_sends, gain_recvs = scratch[9:]
    work.greet()
    for pair in range(4):
        right = grad_cols[:, pair * 256 : pair * 256 + 256]
        product = wide_dot(normed_one_t[...], right)
        if pair == 3:
            lane = lax.broadcasted_iota(jnp.int32, product.shape, 1)
            product = jnp.where(lane < 192, product, wide_dot(attended_t[...], right))
        put_columns(work.parts, 0, 2 * pair, product)
    gain_steps = [[work.core_partner], [work.y_partner], [work.x_partner], work.z_partners]
    gain_steps += [[partner] for partner in work.far_partners]
    tally[0] = gains[...]
    flight = []
    slot = 0
    for t in range(max(len(work.stages), len(gain_steps) + 1)):
        if t < len(work.stages):
            work.advance(0, t)
        if flight:
            total = tally[t - 1]
            for copy, landed in flight:
                copy.wait_recv()
                total = total + from_gain[landed]
            flight = []
            if t < len(gain_steps):
                tally[t] = total
            else:
                out_gains[...] = total
        if t < len(gain_steps):
            for partner in gain_steps[t]:
                copy = remote(
                    tally.at[t], from_gain.at[slot], gain_sends.at[slot], gain_recvs.at[slot], partner
                )
                copy.start()
                work.pending.append(copy)
                flight.append((copy, slot))
                slot += 1
    for t in range(TILES):
        out_cols[:, t * 128 : t * 128 + 128] = work.final[0, t].astype(jnp.float32)
    work.finish()


def reduce_tail(replicas, *operands):
    vmem = pl.BlockSpec(memory_space=pltpu.VMEM)
    wide = jnp.float32
    far = max(replicas.bit_length() - 4, 0)
    return pl.pallas_call(
        functools.partial(tail_kernel, replicas),
        out_shape=[
            jax.ShapeDtypeStruct((144, 1024), wide),
            jax.ShapeDtypeStruct((8, 256), wide),
        ],
        in_specs=[vmem] * len(operands),
        out_specs=[vmem] * 2,
        scratch_shapes=reduction_scratch(replicas, 1)
        + [
            pltpu.VMEM((4 + far, 8, 256), wide),
            pltpu.VMEM((6 + far, 8, 256), wide),
            pltpu.SemaphoreType.DMA((6 + far,)),
            pltpu.SemaphoreType.DMA((6 + far,)),
        ],
        compiler_params=pltpu.CompilerParams(
            collective_id=5, has_side_effects=True, vmem_limit_bytes=VMEM_LIMIT
        ),
    )(*operands)


def per_device(
    inputs,
    seg_ids,
    seq_starts,
    gain_one,
    query_w,
    key_w,
    value_weight,
    out_w,
    gain_two,
    gate_w,
    up_w,
    down_w,
    out_grad,
):
    gains = jnp.stack([gain_one, gain_two])
    gains = jnp.pad(gains, ((0, 14), (0, 256 - gains.shape[1])))
    qkvo_all, gains_all = gather_weights(
        jnp.concatenate([query_w, key_w, value_weight, out_w], axis=1), gains
    )
    qkvo_all = qkvo_all.reshape(4 * query_w.shape[0], qkvo_all.shape[2])
    gain_one_all = gains_all[:, 0, : gain_one.shape[0]].reshape(4 * gain_one.shape[0])
    gain_two_all = gains_all[:, 1, : gain_one.shape[0]].reshape(4 * gain_one.shape[0])
    joined_w = qkvo_all[:, : query_w.shape[1] + 2 * key_w.shape[1]]
    out_all = qkvo_all[:, query_w.shape[1] + 2 * key_w.shape[1] :]
    query_all = qkvo_all[:, : query_w.shape[1]]
    key_all = qkvo_all[:, query_w.shape[1] : query_w.shape[1] + key_w.shape[1]]
    tok_rows = inputs.shape[0]
    query_heads = query_all.shape[1] // HEAD_DIM
    kv_heads = key_all.shape[1] // HEAD_DIM
    repeat_heads = query_heads // kv_heads
    kv_width = kv_heads * HEAD_DIM
    score_scale = 1.0 / math.sqrt(HEAD_DIM)
    reach_back = SEQUENCE_LENGTH // tok_rows
    window_rows = (reach_back + 1) * tok_rows
    device = lax.axis_index(("replica", "group"))
    token_index = device * tok_rows + jnp.arange(tok_rows, dtype=jnp.int32)
    segment_table = jnp.arange(seq_starts.shape[0], dtype=jnp.int32)
    first_token = jnp.sum(
        jnp.where(seg_ids[:, None] == segment_table[None, :], seq_starts[None, :], 0), axis=1
    )
    rotary_angles = rope_angles(token_index - first_token, HEAD_DIM)
    key_index = (device - reach_back) * tok_rows + jnp.arange(window_rows, dtype=jnp.int32)
    inputs_wide = inputs.astype(jnp.float32)
    scale_one = rms_scale(inputs_wide)
    gain_one_wide = gain_one_all.astype(jnp.float32)
    first_normed = (inputs_wide * scale_one * gain_one_wide).astype(jnp.bfloat16)
    projected = jnp.dot(first_normed, joined_w, preferred_element_type=jnp.float32)
    query_cols = query_heads * HEAD_DIM
    queries = apply_rotary(
        projected[:, :query_cols].reshape(tok_rows, query_heads, HEAD_DIM), rotary_angles
    ).astype(jnp.bfloat16)
    key_matrix = apply_rotary(
        projected[:, query_cols : query_cols + kv_width].reshape(tok_rows, kv_heads, HEAD_DIM),
        rotary_angles,
    )
    value_matrix = projected[:, query_cols + kv_width :].astype(jnp.bfloat16)
    packed = jnp.concatenate(
        [
            key_matrix.astype(jnp.bfloat16),
            value_matrix.reshape(tok_rows, kv_heads, HEAD_DIM),
        ],
        axis=2,
    ).reshape(tok_rows, 2 * kv_width)
    bias = jnp.where(
        (key_index[:, None] <= token_index[None, :]) & (key_index[:, None] >= first_token[None, :]),
        0.0,
        masked_score,
    ).reshape(reach_back + 1, tok_rows, tok_rows)
    query_rows = (queries * jnp.bfloat16(score_scale)).reshape(
        tok_rows, kv_heads, repeat_heads, HEAD_DIM
    )
    query_rows = query_rows.transpose(1, 2, 0, 3)
    query_rows = query_rows.reshape(kv_heads, repeat_heads * tok_rows, HEAD_DIM)
    query_rows = jnp.pad(query_rows, ((0, 0), (0, 0), (0, HEAD_DIM)))
    queries_t = query_rows.transpose(0, 2, 1)
    window_blocks, gate_all, up_all, down_all, attended_t, log_total = forward_attention(
        packed, gate_w, up_w, down_w, queries_t, bias
    )
    gate_all, up_all, down_all = (
        a.reshape(a.shape[0] * a.shape[1], a.shape[2]) for a in (gate_all, up_all, down_all)
    )
    attended_wide = attended_t
    attended_t = attended_t.astype(jnp.bfloat16)
    middle = inputs_wide + contract_rows(attended_t, out_all)
    scale_two = rms_scale(middle)
    gain_two_wide = gain_two_all.astype(jnp.float32)
    normed_two = (middle * scale_two * gain_two_wide).astype(jnp.bfloat16)
    gate = jnp.dot(normed_two, gate_all, preferred_element_type=jnp.float32)
    upper = jnp.dot(normed_two, up_all, preferred_element_type=jnp.float32)
    sigmoid_gate = jax.nn.sigmoid(gate)
    hidden = (gate * sigmoid_gate * upper).astype(jnp.bfloat16)
    outputs = middle + jnp.dot(hidden, down_all, preferred_element_type=jnp.float32)
    grad_hidden = times_transpose(out_grad, down_all)
    grad_gate = (grad_hidden * upper * sigmoid_gate * (1.0 + gate * (1.0 - sigmoid_gate))).astype(
        jnp.bfloat16
    )
    grad_up = (grad_hidden * gate * sigmoid_gate).astype(jnp.bfloat16)
    grad_normed_two = times_transpose(grad_gate, gate_all) + times_transpose(grad_up, up_all)
    grad_middle_norm, grad_gain_two = norm_back(grad_normed_two, middle, scale_two, gain_two_wide)
    grad_middle = out_grad.astype(jnp.float32) + grad_middle_norm
    grad_branch = grad_middle.astype(jnp.bfloat16)
    grad_attended_t = times_transpose(out_all, grad_branch).astype(jnp.bfloat16)
    delta = jnp.sum(
        (grad_attended_t.astype(jnp.float32) * attended_wide).reshape(
            query_heads, HEAD_DIM, tok_rows
        ),
        axis=1,
    ).reshape(kv_heads, 1, repeat_heads * tok_rows)
    back_t = grad_attended_t.reshape(kv_heads, repeat_heads, HEAD_DIM, tok_rows)
    back_t = back_t.transpose(0, 2, 1, 3).reshape(kv_heads, HEAD_DIM, repeat_heads * tok_rows)
    back_t = jnp.pad(back_t, ((0, 0), (HEAD_DIM, 0), (0, 0)))
    out_gate, out_up, grad_down_w, out_branch, grad_window, grad_query_t = feed_and_attention_back(
        lax.axis_size("replica"),
        normed_two.T,
        attended_t,
        out_grad.T,
        grad_gate,
        grad_up,
        grad_branch,
        hidden,
        bias,
        window_blocks,
        queries_t,
        back_t,
        query_rows,
        back_t.transpose(0, 2, 1),
        log_total,
        delta,
    )
    grad_query_rot = (
        grad_query_t.reshape(kv_heads, HEAD_DIM, repeat_heads, tok_rows).transpose(3, 0, 2, 1)
        * score_scale
    )
    own_grad = return_window(grad_window).reshape(tok_rows, kv_heads, 2 * HEAD_DIM)
    grad_keys = apply_rotary(own_grad[:, :, :HEAD_DIM], -rotary_angles)
    grad_keys = grad_keys.reshape(tok_rows, kv_width).astype(jnp.bfloat16)
    grad_values = own_grad[:, :, HEAD_DIM:].reshape(tok_rows, kv_width).astype(jnp.bfloat16)
    grad_queries = apply_rotary(
        grad_query_rot.reshape(tok_rows, query_heads, HEAD_DIM), -rotary_angles
    )
    grad_queries = grad_queries.reshape(tok_rows, query_cols).astype(jnp.bfloat16)
    grad_qkv = jnp.concatenate([grad_queries, grad_keys, grad_values], axis=1)
    grad_normed_one = times_transpose(grad_qkv, joined_w)
    grad_inputs_norm, grad_gain_one = norm_back(
        grad_normed_one, inputs_wide, scale_one, gain_one_wide
    )
    grad_inputs = grad_middle + grad_inputs_norm
    width = gain_one_all.shape[0]
    gain_grads = jnp.pad(jnp.concatenate([grad_gain_one, grad_gain_two]), (0, 2048 - 2 * width))
    tail, gain_sums = reduce_tail(
        lax.axis_size("replica"),
        first_normed.T,
        attended_t,
        jnp.concatenate([grad_qkv, grad_branch[:, 512:]], axis=1),
        gain_grads.reshape(8, 256),
    )
    gain_sums = gain_sums.reshape(2048)[: 2 * width].reshape(2, width)
    shard = width // lax.axis_size("group")
    gain_sums = lax.dynamic_slice_in_dim(gain_sums, lax.axis_index("group") * shard, shard, 1)
    first = query_cols
    second = first + kv_width
    third = second + kv_width
    return (
        outputs,
        grad_inputs,
        gain_sums[0],
        tail[:, :first],
        tail[:, first:second],
        tail[:, second:third],
        jnp.concatenate([out_branch, tail[:, third:]], axis=1),
        gain_sums[1],
        out_gate,
        out_up,
        grad_down_w,
    )


def solution(mesh):
    placed = (
        P(("replica", "group"), None),
        P(("replica", "group")),
        P(),
        P("group"),
        P("group", None),
        P("group", None),
        P("group", None),
        P("group", None),
        P("group"),
        P("group", None),
        P("group", None),
        P("group", None),
        P(("replica", "group"), None),
    )
    return jax.shard_map(
        per_device,
        mesh=mesh,
        in_specs=placed,
        out_specs=(
            P(("replica", "group"), None),
            P(("replica", "group"), None),
            P("group"),
            P("group", None),
            P("group", None),
            P("group", None),
            P("group", None),
            P("group"),
            P("group", None),
            P("group", None),
            P("group", None),
        ),
        check_vma=False,
    )
```

```python
import functools
import math

import jax
import jax.numpy as jnp
from jax import lax
from jax.experimental import pallas as pl
from jax.experimental.pallas import tpu as pltpu
from jax.sharding import PartitionSpec as P

HEAD_DIM = 64
SEQUENCE_LENGTH = 2048


epsilon = 1e-05
rope_base = 100000.0
masked_score = -1e30


def from_behind(block, axis, distance):
    devices = range(lax.axis_size(axis))
    route = [(i - distance, i) for i in devices if i - distance in devices]
    return lax.ppermute(block, axis, route)


def rms_scale(value_matrix):
    return lax.rsqrt(jnp.mean(value_matrix * value_matrix, axis=-1, keepdims=True) + epsilon)


def rope_angles(positions, head_size):
    frequency = jnp.exp(
        jnp.arange(0, head_size, 2, dtype=jnp.float32) * (-math.log(rope_base) / head_size)
    )
    return positions.astype(jnp.float32)[:, None] * frequency[None, :]


def apply_rotary(value_matrix, rotary_angles):
    middle_cut = value_matrix.shape[-1] // 2
    former = value_matrix[..., :middle_cut]
    latter = value_matrix[..., middle_cut:]
    cosine = jnp.cos(rotary_angles)[:, None, :]
    sine_part = jnp.sin(rotary_angles)[:, None, :]
    return jnp.concatenate(
        [former * cosine - latter * sine_part, latter * cosine + former * sine_part], axis=-1
    )


def contract_rows(former, latter):
    return lax.dot_general(
        former, latter, (((0,), (0,)), ((), ())), preferred_element_type=jnp.float32
    )


def times_transpose(former, latter):
    return lax.dot_general(
        former, latter, (((1,), (1,)), ((), ())), preferred_element_type=jnp.float32
    )


def norm_back(grad_normed, value_matrix, scale_rows, gain_wide):
    weighted = grad_normed * gain_wide
    cubed = scale_rows * scale_rows * scale_rows
    grad_values = scale_rows * weighted - value_matrix * cubed * jnp.mean(
        weighted * value_matrix, axis=-1, keepdims=True
    )
    grad_gain = jnp.sum(grad_normed * value_matrix * scale_rows, axis=0)
    return (grad_values, grad_gain)


MESH = pl.DeviceIdType.MESH
VMEM_LIMIT = 56 * 1024 * 1024


def flip_bit(index, bit):
    return index + bit - 2 * bit * (lax.rem(lax.div(index, bit), 2))


def greet(partners):
    barrier = pltpu.get_barrier_semaphore()
    for partner in partners:
        pl.semaphore_signal(barrier, inc=1, device_id=partner, device_id_type=MESH)
    pl.semaphore_wait(barrier, len(partners))


def remote(source, target, send_sem, recv_sem, partner):
    return pltpu.make_async_remote_copy(
        src_ref=source,
        dst_ref=target,
        send_sem=send_sem,
        recv_sem=recv_sem,
        device_id=partner,
        device_id_type=MESH,
    )


def half_of(shard, part):
    if shard.shape[-1] % 256 == 0:
        width = shard.shape[-1] // 2
        return shard.at[:, pl.ds(pl.multiple_of(part * width, 128), width)]
    height = shard.shape[-2] // 2
    return shard.at[pl.ds(pl.multiple_of(part * height, 16), height), :]


class Gather:
    def __init__(self, shards, wholes, sends, recvs, local):
        self.shards, self.wholes = shards, wholes
        self.sends, self.recvs, self.local = sends, recvs, local
        r = lax.axis_index("replica")
        self.g = lax.axis_index("group")
        self.x = lax.rem(r, 2)
        self.core_partner = (r, flip_bit(self.g, 1))
        self.y_partner = (r, flip_bit(self.g, 2))
        self.x_partner = (flip_bit(r, 1), self.g)
        self.across = flip_bit(self.g, 2)
        self.from_y, self.from_x, self.full, self.own = [], [], [], []

    def start(self, i, slot, source, target, partner):
        copy = remote(source, target, self.sends.at[i, slot], self.recvs.at[i, slot], partner)
        copy.start()
        return copy

    def begin(self):
        for i, (shard, whole) in enumerate(zip(self.shards, self.wholes)):
            self.from_y.append(
                self.start(
                    i,
                    0,
                    half_of(shard, self.x),
                    half_of(whole.at[self.g], self.x),
                    self.y_partner,
                )
            )
        for i, (shard, whole) in enumerate(zip(self.shards, self.wholes)):
            self.full.append(self.start(i, 1, shard, whole.at[self.g], self.core_partner))
            own = pltpu.make_async_copy(shard, whole.at[self.g], self.local.at[i])
            own.start()
            self.own.append(own)

    def pass_y(self, *chosen):
        for i in chosen:
            whole = self.wholes[i]
            self.from_y[i].wait_recv()
            piece = half_of(whole.at[self.across], self.x)
            self.from_x.append(self.start(i, 2, piece, piece, self.x_partner))
            self.full.append(self.start(i, 3, piece, piece, self.core_partner))

    def pass_x(self, *chosen):
        for i in chosen:
            whole = self.wholes[i]
            self.from_x[i].wait_recv()
            piece = half_of(whole.at[self.across], 1 - self.x)
            self.full.append(self.start(i, 4, piece, piece, self.core_partner))

    def finish(self):
        for copy in self.own + self.full:
            copy.wait()
        for copy in self.from_y + self.from_x:
            copy.wait_send()


def gather_kernel(count, *refs):
    work = Gather(refs[:count], refs[count : 2 * count], *refs[2 * count :])
    greet((work.core_partner, work.y_partner, work.x_partner))
    work.begin()
    work.pass_y(*range(count))
    work.pass_x(*range(count))
    work.finish()


def gather_scratch(count):
    return [
        pltpu.SemaphoreType.DMA((count, 5)),
        pltpu.SemaphoreType.DMA((count, 5)),
        pltpu.SemaphoreType.DMA((count,)),
    ]


def gather_weights(*arrays):
    vmem = pl.BlockSpec(memory_space=pltpu.VMEM)
    return pl.pallas_call(
        functools.partial(gather_kernel, len(arrays)),
        out_shape=[jax.ShapeDtypeStruct((4,) + a.shape, a.dtype) for a in arrays],
        in_specs=[vmem] * len(arrays),
        out_specs=[vmem] * len(arrays),
        scratch_shapes=gather_scratch(len(arrays)),
        compiler_params=pltpu.CompilerParams(
            collective_id=1, has_side_effects=True, vmem_limit_bytes=VMEM_LIMIT
        ),
    )(*arrays)


def place():
    r = lax.axis_index("replica")
    g = lax.axis_index("group")
    slabs = lax.axis_size("replica") // 2
    slab = lax.div(r, 2)
    return r, g, slabs, slab


def slot_of(block, here):
    return lax.rem(block - here + 8, 8)


def forward_kernel(
    packed,
    gate,
    up,
    down,
    queries_t,
    bias_t,
    window,
    gate_all,
    up_all,
    down_all,
    attended_t,
    log_total,
    peak,
    sums,
    mixed,
    sends,
    recvs,
    local,
    *gather_refs,
):
    r, g, slabs, slab = place()
    x = lax.rem(r, 2)
    y = lax.div(g, 2)
    c = lax.rem(g, 2)
    rx, gy, gc = flip_bit(r, 1), flip_bit(g, 2), flip_bit(g, 1)
    here = x * 4 + g
    at_x, at_y, at_c = (1 - x) * 4 + g, x * 4 + gy, x * 4 + gc
    at_xy = (1 - x) * 4 + gy
    far_x, far_y = (1 - x) * 4 + gc, x * 4 + flip_bit(gc, 2)
    far_xy = (1 - x) * 4 + flip_bit(gc, 2)
    ahead = (2 * lax.rem(slab + 1, slabs) + x, g)
    behind = (2 * lax.rem(slab + slabs - 1, slabs) + x, g)
    barrier = pltpu.get_barrier_semaphore()
    for partner in ((rx, g), (r, gy), (r, gc), behind):
        pl.semaphore_signal(barrier, inc=1, device_id=partner, device_id_type=MESH)
    pl.semaphore_wait(barrier, 4)
    weights = Gather((gate, up, down), (gate_all, up_all, down_all), *gather_refs)
    to_ahead = remote(packed, window.at[0], sends.at[0], recvs.at[0], ahead)
    to_ahead.start()
    firsts = []
    for i, (bit, partner, there) in enumerate(
        ((x, (rx, g), at_x), (y, (r, gy), at_y), (c, (r, gc), at_c))
    ):
        target = window.at[slot_of(here, there)]
        early = remote(packed, target, sends.at[1 + i], recvs.at[1 + i], partner)
        late = remote(window.at[0], target, sends.at[1 + i], recvs.at[1 + i], partner)
        firsts.append((bit, early, late))
    for bit, early, late in firsts:
        pl.when(bit == 0)(early.start)
    own = pltpu.make_async_copy(packed, window.at[8], local)
    own.start()
    weights.begin()

    def attend(slot, first=False):
        for head in range(3):
            kv = window[slot, :, head * 128 : head * 128 + 128]
            bias = bias_t[slot]
            scores = wide_dot(kv, queries_t[head]) + jnp.concatenate([bias, bias, bias], axis=1)
            top = jnp.max(scores, axis=0, keepdims=True)
            if not first:
                before = peak[head]
                top = jnp.maximum(before, top)
                fade = jnp.exp(before - top)
            exponent = jnp.exp(scores - top)
            part = jnp.sum(exponent, axis=0, keepdims=True)
            block = contract_rows(kv, exponent.astype(jnp.bfloat16))
            peak[head] = top
            if first:
                sums[head] = part
                mixed[head] = block
            else:
                sums[head] = sums[head] * fade + part
                mixed[head] = mixed[head] * fade + block

    own.wait()
    attend(8, True)
    to_ahead.wait_recv()
    for bit, early, late in firsts:
        pl.when(bit == 1)(late.start)
    attend(0)
    firsts[0][1].wait_recv()
    slot_x = window.at[slot_of(at_x, here)]
    diagonal = remote(
        slot_x, window.at[slot_of(at_x, at_y)], sends.at[4], recvs.at[4], (r, gy)
    )
    diagonal.start()
    core_x = remote(slot_x, window.at[slot_of(at_x, at_c)], sends.at[5], recvs.at[5], (r, gc))
    core_x.start()
    firsts[1][1].wait_recv()
    slot_y = window.at[slot_of(at_y, here)]
    core_y = remote(slot_y, window.at[slot_of(at_y, at_c)], sends.at[6], recvs.at[6], (r, gc))
    core_y.start()
    attend(slot_of(at_x, here))
    weights.pass_y(0)
    attend(slot_of(at_y, here))
    weights.pass_y(1)
    diagonal.wait_recv()
    slot_xy = window.at[slot_of(at_xy, here)]
    core_xy = remote(slot_xy, window.at[slot_of(at_xy, at_c)], sends.at[7], recvs.at[7], (r, gc))
    core_xy.start()
    attend(slot_of(at_xy, here))
    weights.pass_y(2)
    firsts[2][1].wait_recv()
    attend(slot_of(at_c, here))
    weights.pass_x(0)
    core_x.wait_recv()
    attend(slot_of(far_x, here))
    weights.pass_x(1)
    core_y.wait_recv()
    attend(slot_of(far_y, here))
    weights.pass_x(2)
    core_xy.wait_recv()
    attend(slot_of(far_xy, here))
    for head in range(3):
        out = mixed[head][64:] / sums[head]
        for row in range(3):
            spot = (head * 3 + row) * 64
            attended_t[spot : spot + 64, :] = out[:, row * 256 : row * 256 + 256]
        log_total[head] = peak[head] + jnp.log(sums[head])
    weights.finish()
    for copy in (to_ahead, firsts[0][1], firsts[1][1], firsts[2][1], diagonal, core_x, core_y, core_xy):
        copy.wait_send()


def forward_attention(packed, gate, up, down, queries_t, bias_t):
    vmem = pl.BlockSpec(memory_space=pltpu.VMEM)
    wide = jnp.float32
    shapes = [jax.ShapeDtypeStruct((9,) + packed.shape, packed.dtype)]
    shapes += [jax.ShapeDtypeStruct((4,) + a.shape, a.dtype) for a in (gate, up, down)]
    shapes += [
        jax.ShapeDtypeStruct((576, 256), wide),
        jax.ShapeDtypeStruct((3, 1, 768), wide),
    ]
    return pl.pallas_call(
        forward_kernel,
        out_shape=shapes,
        in_specs=[vmem] * 6,
        out_specs=[vmem] * len(shapes),
        scratch_shapes=[
            pltpu.VMEM((3, 1, 768), wide),
            pltpu.VMEM((3, 1, 768), wide),
            pltpu.VMEM((3, 128, 768), wide),
            pltpu.SemaphoreType.DMA((8,)),
            pltpu.SemaphoreType.DMA((8,)),
            pltpu.SemaphoreType.DMA,
        ]
        + gather_scratch(3),
        compiler_params=pltpu.CompilerParams(
            collective_id=2, has_side_effects=True, vmem_limit_bytes=VMEM_LIMIT
        ),
    )(packed, gate, up, down, queries_t, bias_t)


def return_kernel(window, total, outgoing, landed, sums, sends, recvs):
    r, g, slabs, slab = place()
    x = lax.rem(r, 2)
    y = lax.div(g, 2)
    c = lax.rem(g, 2)
    rx, gy, gc = flip_bit(r, 1), flip_bit(g, 2), flip_bit(g, 1)
    here = x * 4 + g
    at_x, at_y, at_c = (1 - x) * 4 + g, x * 4 + gy, x * 4 + gc
    at_xy = (1 - x) * 4 + gy
    far = [x * 4 + gc, x * 4 + flip_bit(gc, 2), (1 - x) * 4 + gc, (1 - x) * 4 + flip_bit(gc, 2)]
    ahead = (2 * lax.rem(slab + 1, slabs) + x, g)
    behind = (2 * lax.rem(slab + slabs - 1, slabs) + x, g)
    barrier = pltpu.get_barrier_semaphore()
    for partner in ((rx, g), (r, gy), (r, gc), ahead):
        pl.semaphore_signal(barrier, inc=1, device_id=partner, device_id_type=MESH)
    pl.semaphore_wait(barrier, 4)
    wide = jnp.float32
    low = jnp.bfloat16
    core = []
    for i in (3, 1, 2, 0):
        copy = remote(
            window.at[slot_of(far[i], here)], landed.at[i], sends.at[i], recvs.at[i], (r, gc)
        )
        copy.start()
        core.append(copy)

    def blend(bit, index):
        block = landed[index].astype(wide)
        zero = jnp.zeros_like(block)
        total[...] += jnp.where(bit == 0, block, zero)
        sums[...] += jnp.where(bit == 1, block, zero)

    core[0].wait_recv()
    outgoing[0] = (window[slot_of(at_xy, here)].astype(wide) + landed[3].astype(wide)).astype(low)
    to_y_diagonal = remote(outgoing.at[0], landed.at[4], sends.at[4], recvs.at[4], (r, gy))
    to_y_diagonal.start()
    core[1].wait_recv()
    outgoing[1] = (window[slot_of(at_y, here)].astype(wide) + landed[1].astype(wide)).astype(low)
    to_y = remote(outgoing.at[1], landed.at[5], sends.at[5], recvs.at[5], (r, gy))
    to_y.start()
    core[2].wait_recv()
    to_y_diagonal.wait_recv()
    outgoing[2] = (
        window[slot_of(at_x, here)].astype(wide) + landed[2].astype(wide) + landed[4].astype(wide)
    ).astype(low)
    to_x = remote(outgoing.at[2], landed.at[6], sends.at[6], recvs.at[6], (rx, g))
    to_x.start()
    total[...] = window[8].astype(wide)
    sums[...] = window[0].astype(wide)
    core[3].wait_recv()
    blend(c, 0)
    to_y.wait_recv()
    blend(y, 5)
    to_x.wait_recv()
    blend(x, 6)
    outgoing[3] = sums[...].astype(low)
    to_behind = remote(outgoing.at[3], landed.at[7], sends.at[7], recvs.at[7], behind)
    to_behind.start()
    to_behind.wait_recv()
    total[...] += landed[7].astype(wide)
    for copy in core + [to_y_diagonal, to_y, to_x, to_behind]:
        copy.wait_send()


def return_window(window):
    block = window.shape[1:]
    vmem = pl.BlockSpec(memory_space=pltpu.VMEM)
    return pl.pallas_call(
        return_kernel,
        out_shape=jax.ShapeDtypeStruct(block, jnp.float32),
        in_specs=[vmem],
        out_specs=vmem,
        scratch_shapes=[
            pltpu.VMEM((4,) + block, window.dtype),
            pltpu.VMEM((8,) + block, window.dtype),
            pltpu.VMEM(block, jnp.float32),
            pltpu.SemaphoreType.DMA((8,)),
            pltpu.SemaphoreType.DMA((8,)),
        ],
        compiler_params=pltpu.CompilerParams(
            collective_id=3, has_side_effects=True, vmem_limit_bytes=VMEM_LIMIT
        ),
    )(window)


TILES = 8


class Reduction:
    def __init__(self, replicas, chunks, buffers, sends, recvs):
        (
            self.parts,
            self.from_core,
            self.from_y,
            self.from_x,
            self.from_z,
            self.from_far,
            self.final,
        ) = buffers
        self.sends, self.recvs = sends, recvs
        r = lax.axis_index("replica")
        g = lax.axis_index("group")
        self.c, self.y, self.x = lax.rem(g, 2), lax.div(g, 2), lax.rem(r, 2)
        self.z = lax.rem(lax.div(r, 2), 4)
        base = r - 2 * self.z
        self.core_partner = (r, flip_bit(g, 1))
        self.y_partner = (r, flip_bit(g, 2))
        self.x_partner = (flip_bit(r, 1), g)
        self.z_partners = [(base + 2 * lax.rem(self.z + d, 4), g) for d in (1, 2, 3)]
        self.far_partners = []
        bit = 8
        while bit < replicas:
            self.far_partners.append((flip_bit(r, bit), g))
            bit *= 2
        self.pending = []
        self.stages = (
            self.stage_core,
            self.stage_y,
            self.stage_x,
            self.stage_z,
            self.stage_back,
            self.stage_back_x,
            self.stage_end,
        )
        self.state = [None] * chunks

    def greet(self):
        greet(
            [self.core_partner, self.y_partner, self.x_partner] + self.z_partners + self.far_partners
        )

    def advance(self, chunk, stage):
        self.state[chunk] = self.stages[stage](chunk, self.state[chunk])

    def start(self, chunk, slot, source, target, partner):
        copy = remote(source, target, self.sends.at[chunk, slot], self.recvs.at[chunk, slot], partner)
        copy.start()
        self.pending.append(copy)
        return copy

    def finish(self):
        for copy in self.pending:
            copy.wait_send()

    def stage_core(self, k, arrived):
        return self.start(
            k, 0, self.parts.at[1 - self.c, :, k], self.from_core.at[k], self.core_partner
        )

    def stage_y(self, k, arrived):
        arrived.wait_recv()
        parts, c = self.parts, self.c

        def add(t, carry):
            for yy in range(2):
                parts[c, yy, k, t] = (
                    parts[c, yy, k, t].astype(jnp.float32)
                    + self.from_core[k, yy, t].astype(jnp.float32)
                ).astype(jnp.bfloat16)
            return carry

        lax.fori_loop(0, TILES, add, 0)
        return self.start(k, 1, parts.at[c, 1 - self.y, k], self.from_y.at[k], self.y_partner)

    def stage_x(self, k, arrived):
        arrived.wait_recv()
        parts, c, y, x = self.parts, self.c, self.y, self.x
        half = TILES // 2

        def add(t, carry):
            parts[c, y, k, t] = (
                parts[c, y, k, t].astype(jnp.float32) + self.from_y[k, t].astype(jnp.float32)
            ).astype(jnp.bfloat16)
            return carry

        lax.fori_loop(0, TILES, add, 0)
        return self.start(
            k, 2, parts.at[c, y, k, pl.ds((1 - x) * half, half)], self.from_x.at[k], self.x_partner
        )

    def stage_z(self, k, arrived):
        arrived.wait_recv()
        parts, c, y, x = self.parts, self.c, self.y, self.x
        half = TILES // 2

        def add(t, carry):
            parts[c, y, k, x * half + t] = (
                parts[c, y, k, x * half + t].astype(jnp.float32)
                + self.from_x[k, t].astype(jnp.float32)
            ).astype(jnp.bfloat16)
            return carry

        lax.fori_loop(0, half, add, 0)
        return [
            self.start(
                k,
                2 + d,
                parts.at[c, y, k, x * half + lax.rem(self.z + d, 4)],
                self.from_z.at[k, d - 1],
                self.z_partners[d - 1],
            )
            for d in range(1, 4)
        ]

    def stage_back(self, k, arrived):
        for copy in arrived:
            copy.wait_recv()
        final = self.final
        spot = self.x * (TILES // 2) + self.z
        total = self.parts[self.c, self.y, k, spot].astype(jnp.float32)
        for d in range(3):
            total = total + self.from_z[k, d].astype(jnp.float32)
        for step, partner in enumerate(self.far_partners):
            self.from_far[k, 2 * step] = total.astype(jnp.bfloat16)
            copy = self.start(
                k,
                9 + step,
                self.from_far.at[k, 2 * step],
                self.from_far.at[k, 2 * step + 1],
                partner,
            )
            copy.wait_recv()
            total = total + self.from_far[k, 2 * step + 1].astype(jnp.float32)
        final[k, spot] = total.astype(jnp.bfloat16)
        own = final.at[k, spot]
        return [self.start(k, 5 + d, own, own, self.z_partners[d - 1]) for d in range(1, 4)]

    def stage_back_x(self, k, arrived):
        for copy in arrived:
            copy.wait_recv()
        own = self.final.at[k, pl.ds(self.x * (TILES // 2), TILES // 2)]
        return self.start(k, 9 + len(self.far_partners), own, own, self.x_partner)

    def stage_end(self, k, arrived):
        arrived.wait_recv()


def reduction_scratch(replicas, chunks):
    far = max(replicas.bit_length() - 4, 0)
    tile = (144, 128)
    low = jnp.bfloat16
    return [
        pltpu.VMEM((2, 2, chunks, TILES) + tile, low),
        pltpu.VMEM((chunks, 2, TILES) + tile, low),
        pltpu.VMEM((chunks, TILES) + tile, low),
        pltpu.VMEM((chunks, TILES // 2) + tile, low),
        pltpu.VMEM((chunks, 3) + tile, low),
        pltpu.VMEM((chunks, 2 * max(far, 1)) + tile, low),
        pltpu.VMEM((chunks, TILES) + tile, low),
        pltpu.SemaphoreType.DMA((chunks, 10 + far)),
        pltpu.SemaphoreType.DMA((chunks, 10 + far)),
    ]


def put_columns(parts, chunk, tile, product):
    product = product.astype(jnp.bfloat16)
    for s in range(4):
        rows = product[144 * s : 144 * s + 144]
        for j in range(product.shape[1] // 128):
            parts[s % 2, s // 2, chunk, tile + j] = rows[:, j * 128 : j * 128 + 128]


def wide_dot(left, right):
    return jnp.dot(left, right, preferred_element_type=jnp.float32)


FEED_CHUNKS = 5


def feed_kernel(
    replicas,
    normed_two_t,
    attended_t,
    out_grad_t,
    grad_gate,
    grad_up,
    grad_branch,
    hidden,
    bias_t,
    window,
    queries_t,
    grad_attended_t,
    queries_rows,
    grad_attended_rows,
    log_total,
    delta,
    out_gate,
    out_up,
    out_down,
    out_branch,
    grad_window,
    grad_queries_t,
    *scratch,
):
    work = Reduction(replicas, FEED_CHUNKS, scratch[:7], scratch[7], scratch[8])
    parts, final = work.parts, work.final
    work.greet()

    def down_part(chunk, tile, j):
        for s in range(4):
            columns = slice(s * 384 + j * 128, s * 384 + j * 128 + 128)
            product = wide_dot(out_grad_t[...], hidden[:, columns]).astype(jnp.bfloat16)
            for row in range(4):
                parts[s % 2, s // 2, chunk, tile + row] = product[144 * row : 144 * row + 144]

    def columns_part(chunk, tile, left, right, first, last):
        for column in range(first, last, 256):
            put_columns(
                parts,
                chunk,
                tile + (column - first) // 128,
                wide_dot(left[...], right[:, column : column + 256]),
            )

    def products(k):
        if k == 0:
            columns_part(0, 0, normed_two_t, grad_gate, 0, 1024)
        elif k == 1:
            columns_part(1, 0, normed_two_t, grad_gate, 1024, 1536)
            columns_part(1, 4, normed_two_t, grad_up, 0, 512)
        elif k == 2:
            columns_part(2, 0, normed_two_t, grad_up, 512, 1536)
        elif k == 3:
            down_part(3, 0, 0)
            down_part(3, 4, 1)
        else:
            down_part(4, 0, 2)
            columns_part(4, 4, attended_t, grad_branch, 0, 512)

    def write_out(k):
        def columns(target, column, first, count):
            for t in range(count):
                target[:, column + t * 128 : column + t * 128 + 128] = final[k, first + t].astype(
                    jnp.float32
                )

        def rows(first, j):
            block = jnp.concatenate(
                [final[k, first + row].astype(jnp.float32) for row in range(4)], axis=0
            )
            out_down[j * 128 : j * 128 + 128, :] = block.T

        if k == 0:
            columns(out_gate, 0, 0, 8)
        elif k == 1:
            columns(out_gate, 1024, 0, 4)
            columns(out_up, 0, 4, 4)
        elif k == 2:
            columns(out_up, 512, 0, 8)
        elif k == 3:
            rows(0, 0)
            rows(4, 1)
        else:
            rows(0, 2)
            columns(out_branch, 0, 4, 4)

    def attend(c, third):
        lanes = slice(c * 128, c * 128 + 128)
        q_t = queries_t[c]
        a_t = grad_attended_t[c]

        def block(i, carry):
            slot = third * 3 + i
            kv = window[slot, :, lanes]
            bias = bias_t[slot]
            bias = jnp.concatenate([bias, bias, bias], axis=1)
            probs = jnp.exp(wide_dot(kv, q_t) + bias - log_total[c])
            grads = probs * (wide_dot(kv, a_t) - delta[c])
            grads = grads.astype(jnp.bfloat16)
            back = wide_dot(grads, queries_rows[c]) + wide_dot(
                probs.astype(jnp.bfloat16), grad_attended_rows[c]
            )
            grad_window[slot, :, lanes] = back.astype(jnp.bfloat16)
            return carry + contract_rows(kv, grads)

        start = jnp.zeros((128, 768), jnp.float32)
        done = lax.fori_loop(0, 3, block, start)
        if third == 0:
            grad_queries_t[c] = done[:64]
        else:
            grad_queries_t[c] += done[:64]

    last = len(work.stages) - 1
    for t in range(FEED_CHUNKS + last):
        for k in range(FEED_CHUNKS):
            stage = t - k
            if stage == 0:
                products(k)
            if 0 <= stage <= last:
                work.advance(k, stage)
            if stage == last:
                write_out(k)
        if 2 <= t < 11:
            attend((t - 2) // 3, (t - 2) % 3)
    work.finish()


def feed_and_attention_back(replicas, *operands):
    vmem = pl.BlockSpec(memory_space=pltpu.VMEM)
    wide = jnp.float32
    shapes = [
        jax.ShapeDtypeStruct((144, 1536), wide),
        jax.ShapeDtypeStruct((144, 1536), wide),
        jax.ShapeDtypeStruct((384, 576), wide),
        jax.ShapeDtypeStruct((144, 512), wide),
        jax.ShapeDtypeStruct((9, 256, 384), jnp.bfloat16),
        jax.ShapeDtypeStruct((3, 64, 768), wide),
    ]
    return pl.pallas_call(
        functools.partial(feed_kernel, replicas),
        out_shape=shapes,
        in_specs=[vmem] * len(operands),
        out_specs=[vmem] * len(shapes),
        scratch_shapes=reduction_scratch(replicas, FEED_CHUNKS),
        compiler_params=pltpu.CompilerParams(
            collective_id=4, has_side_effects=True, vmem_limit_bytes=VMEM_LIMIT
        ),
    )(*operands)


def tail_kernel(
    replicas,
    normed_one_t,
    attended_t,
    grad_cols,
    gains,
    branch,
    out_query,
    out_key,
    out_value,
    out_branch,
    out_gains,
    *scratch,
):
    work = Reduction(replicas, 1, scratch[:7], scratch[7], scratch[8])
    tally, from_gain, gain_sends, gain_recvs = scratch[9:]
    work.greet()
    for pair in range(4):
        right = grad_cols[:, pair * 256 : pair * 256 + 256]
        product = wide_dot(normed_one_t[...], right)
        if pair == 3:
            lane = lax.broadcasted_iota(jnp.int32, product.shape, 1)
            product = jnp.where(lane < 192, product, wide_dot(attended_t[...], right))
        put_columns(work.parts, 0, 2 * pair, product)
    gain_steps = [[work.core_partner], [work.y_partner], [work.x_partner], work.z_partners]
    gain_steps += [[partner] for partner in work.far_partners]
    tally[0] = gains[...]
    flight = []
    slot = 0
    for t in range(max(len(work.stages), len(gain_steps) + 1)):
        if t < len(work.stages):
            work.advance(0, t)
        if flight:
            total = tally[t - 1]
            for copy, landed in flight:
                copy.wait_recv()
                total = total + from_gain[landed]
            flight = []
            if t < len(gain_steps):
                tally[t] = total
            else:
                out_gains[...] = total
        if t < len(gain_steps):
            for partner in gain_steps[t]:
                copy = remote(
                    tally.at[t], from_gain.at[slot], gain_sends.at[slot], gain_recvs.at[slot], partner
                )
                copy.start()
                work.pending.append(copy)
                flight.append((copy, slot))
                slot += 1
    columns = jnp.concatenate(
        [work.final[0, t].astype(jnp.float32) for t in range(TILES)], axis=1
    )
    out_query[...] = columns[:, :576]
    out_key[...] = columns[:, 576:768]
    out_value[...] = columns[:, 768:960]
    out_branch[:, :512] = branch[...]
    out_branch[:, 512:] = columns[:, 960:]
    work.finish()


def reduce_tail(replicas, *operands):
    vmem = pl.BlockSpec(memory_space=pltpu.VMEM)
    wide = jnp.float32
    far = max(replicas.bit_length() - 4, 0)
    return pl.pallas_call(
        functools.partial(tail_kernel, replicas),
        out_shape=[
            jax.ShapeDtypeStruct((144, 576), wide),
            jax.ShapeDtypeStruct((144, 192), wide),
            jax.ShapeDtypeStruct((144, 192), wide),
            jax.ShapeDtypeStruct((144, 576), wide),
            jax.ShapeDtypeStruct((8, 256), wide),
        ],
        in_specs=[vmem] * len(operands),
        out_specs=[vmem] * 5,
        scratch_shapes=reduction_scratch(replicas, 1)
        + [
            pltpu.VMEM((4 + far, 8, 256), wide),
            pltpu.VMEM((6 + far, 8, 256), wide),
            pltpu.SemaphoreType.DMA((6 + far,)),
            pltpu.SemaphoreType.DMA((6 + far,)),
        ],
        compiler_params=pltpu.CompilerParams(
            collective_id=5, has_side_effects=True, vmem_limit_bytes=VMEM_LIMIT
        ),
    )(*operands)


def per_device(
    inputs,
    seg_ids,
    seq_starts,
    gain_one,
    query_w,
    key_w,
    value_weight,
    out_w,
    gain_two,
    gate_w,
    up_w,
    down_w,
    out_grad,
):
    gains = jnp.stack([gain_one, gain_two])
    gains = jnp.pad(gains, ((0, 14), (0, 256 - gains.shape[1])))
    qkvo_all, gains_all = gather_weights(
        jnp.concatenate([query_w, key_w, value_weight, out_w], axis=1), gains
    )
    qkvo_all = qkvo_all.reshape(4 * query_w.shape[0], qkvo_all.shape[2])
    gain_one_all = gains_all[:, 0, : gain_one.shape[0]].reshape(4 * gain_one.shape[0])
    gain_two_all = gains_all[:, 1, : gain_one.shape[0]].reshape(4 * gain_one.shape[0])
    joined_w = qkvo_all[:, : query_w.shape[1] + 2 * key_w.shape[1]]
    out_all = qkvo_all[:, query_w.shape[1] + 2 * key_w.shape[1] :]
    query_all = qkvo_all[:, : query_w.shape[1]]
    key_all = qkvo_all[:, query_w.shape[1] : query_w.shape[1] + key_w.shape[1]]
    tok_rows = inputs.shape[0]
    query_heads = query_all.shape[1] // HEAD_DIM
    kv_heads = key_all.shape[1] // HEAD_DIM
    repeat_heads = query_heads // kv_heads
    kv_width = kv_heads * HEAD_DIM
    score_scale = 1.0 / math.sqrt(HEAD_DIM)
    reach_back = SEQUENCE_LENGTH // tok_rows
    window_rows = (reach_back + 1) * tok_rows
    device = lax.axis_index(("replica", "group"))
    token_index = device * tok_rows + jnp.arange(tok_rows, dtype=jnp.int32)
    segment_table = jnp.arange(seq_starts.shape[0], dtype=jnp.int32)
    first_token = jnp.sum(
        jnp.where(seg_ids[:, None] == segment_table[None, :], seq_starts[None, :], 0), axis=1
    )
    rotary_angles = rope_angles(token_index - first_token, HEAD_DIM)
    key_index = (device - reach_back) * tok_rows + jnp.arange(window_rows, dtype=jnp.int32)
    inputs_wide = inputs.astype(jnp.float32)
    scale_one = rms_scale(inputs_wide)
    gain_one_wide = gain_one_all.astype(jnp.float32)
    first_normed = (inputs_wide * scale_one * gain_one_wide).astype(jnp.bfloat16)
    projected = jnp.dot(first_normed, joined_w, preferred_element_type=jnp.float32)
    query_cols = query_heads * HEAD_DIM
    queries = apply_rotary(
        projected[:, :query_cols].reshape(tok_rows, query_heads, HEAD_DIM), rotary_angles
    ).astype(jnp.bfloat16)
    key_matrix = apply_rotary(
        projected[:, query_cols : query_cols + kv_width].reshape(tok_rows, kv_heads, HEAD_DIM),
        rotary_angles,
    )
    value_matrix = projected[:, query_cols + kv_width :].astype(jnp.bfloat16)
    packed = jnp.concatenate(
        [
            key_matrix.astype(jnp.bfloat16),
            value_matrix.reshape(tok_rows, kv_heads, HEAD_DIM),
        ],
        axis=2,
    ).reshape(tok_rows, 2 * kv_width)
    bias = jnp.where(
        (key_index[:, None] <= token_index[None, :]) & (key_index[:, None] >= first_token[None, :]),
        0.0,
        masked_score,
    ).reshape(reach_back + 1, tok_rows, tok_rows)
    query_rows = (queries * jnp.bfloat16(score_scale)).reshape(
        tok_rows, kv_heads, repeat_heads, HEAD_DIM
    )
    query_rows = query_rows.transpose(1, 2, 0, 3)
    query_rows = query_rows.reshape(kv_heads, repeat_heads * tok_rows, HEAD_DIM)
    query_rows = jnp.pad(query_rows, ((0, 0), (0, 0), (0, HEAD_DIM)))
    queries_t = query_rows.transpose(0, 2, 1)
    window_blocks, gate_all, up_all, down_all, attended_t, log_total = forward_attention(
        packed, gate_w, up_w, down_w, queries_t, bias
    )
    gate_all, up_all, down_all = (
        a.reshape(a.shape[0] * a.shape[1], a.shape[2]) for a in (gate_all, up_all, down_all)
    )
    attended_wide = attended_t
    attended_t = attended_t.astype(jnp.bfloat16)
    middle = inputs_wide + contract_rows(attended_t, out_all)
    scale_two = rms_scale(middle)
    gain_two_wide = gain_two_all.astype(jnp.float32)
    normed_two = (middle * scale_two * gain_two_wide).astype(jnp.bfloat16)
    gate = jnp.dot(normed_two, gate_all, preferred_element_type=jnp.float32)
    upper = jnp.dot(normed_two, up_all, preferred_element_type=jnp.float32)
    sigmoid_gate = jax.nn.sigmoid(gate)
    hidden = (gate * sigmoid_gate * upper).astype(jnp.bfloat16)
    outputs = middle + jnp.dot(hidden, down_all, preferred_element_type=jnp.float32)
    grad_hidden = times_transpose(out_grad, down_all)
    grad_gate = (grad_hidden * upper * sigmoid_gate * (1.0 + gate * (1.0 - sigmoid_gate))).astype(
        jnp.bfloat16
    )
    grad_up = (grad_hidden * gate * sigmoid_gate).astype(jnp.bfloat16)
    grad_normed_two = times_transpose(grad_gate, gate_all) + times_transpose(grad_up, up_all)
    grad_middle_norm, grad_gain_two = norm_back(grad_normed_two, middle, scale_two, gain_two_wide)
    grad_middle = out_grad.astype(jnp.float32) + grad_middle_norm
    grad_branch = grad_middle.astype(jnp.bfloat16)
    grad_attended_t = times_transpose(out_all, grad_branch).astype(jnp.bfloat16)
    delta = jnp.sum(
        (grad_attended_t.astype(jnp.float32) * attended_wide).reshape(
            query_heads, HEAD_DIM, tok_rows
        ),
        axis=1,
    ).reshape(kv_heads, 1, repeat_heads * tok_rows)
    back_t = grad_attended_t.reshape(kv_heads, repeat_heads, HEAD_DIM, tok_rows)
    back_t = back_t.transpose(0, 2, 1, 3).reshape(kv_heads, HEAD_DIM, repeat_heads * tok_rows)
    back_t = jnp.pad(back_t, ((0, 0), (HEAD_DIM, 0), (0, 0)))
    out_gate, out_up, grad_down_w, out_branch, grad_window, grad_query_t = feed_and_attention_back(
        lax.axis_size("replica"),
        normed_two.T,
        attended_t,
        out_grad.T,
        grad_gate,
        grad_up,
        grad_branch,
        hidden,
        bias,
        window_blocks,
        queries_t,
        back_t,
        query_rows,
        back_t.transpose(0, 2, 1),
        log_total,
        delta,
    )
    grad_query_rot = (
        grad_query_t.reshape(kv_heads, HEAD_DIM, repeat_heads, tok_rows).transpose(3, 0, 2, 1)
        * score_scale
    )
    own_grad = return_window(grad_window).reshape(tok_rows, kv_heads, 2 * HEAD_DIM)
    grad_keys = apply_rotary(own_grad[:, :, :HEAD_DIM], -rotary_angles)
    grad_keys = grad_keys.reshape(tok_rows, kv_width).astype(jnp.bfloat16)
    grad_values = own_grad[:, :, HEAD_DIM:].reshape(tok_rows, kv_width).astype(jnp.bfloat16)
    grad_queries = apply_rotary(
        grad_query_rot.reshape(tok_rows, query_heads, HEAD_DIM), -rotary_angles
    )
    grad_queries = grad_queries.reshape(tok_rows, query_cols).astype(jnp.bfloat16)
    grad_qkv = jnp.concatenate([grad_queries, grad_keys, grad_values], axis=1)
    grad_normed_one = times_transpose(grad_qkv, joined_w)
    grad_inputs_norm, grad_gain_one = norm_back(
        grad_normed_one, inputs_wide, scale_one, gain_one_wide
    )
    grad_inputs = grad_middle + grad_inputs_norm
    width = gain_one_all.shape[0]
    gain_grads = jnp.pad(jnp.concatenate([grad_gain_one, grad_gain_two]), (0, 2048 - 2 * width))
    grad_query_w, grad_key_w, grad_value_w, grad_out_w, gain_sums = reduce_tail(
        lax.axis_size("replica"),
        first_normed.T,
        attended_t,
        jnp.concatenate([grad_qkv, grad_branch[:, 512:]], axis=1),
        gain_grads.reshape(8, 256),
        out_branch,
    )
    gain_sums = gain_sums.reshape(2048)[: 2 * width].reshape(2, width)
    shard = width // lax.axis_size("group")
    gain_sums = lax.dynamic_slice_in_dim(gain_sums, lax.axis_index("group") * shard, shard, 1)
    return (
        outputs,
        grad_inputs,
        gain_sums[0],
        grad_query_w,
        grad_key_w,
        grad_value_w,
        grad_out_w,
        gain_sums[1],
        out_gate,
        out_up,
        grad_down_w,
    )


def solution(mesh):
    placed = (
        P(("replica", "group"), None),
        P(("replica", "group")),
        P(),
        P("group"),
        P("group", None),
        P("group", None),
        P("group", None),
        P("group", None),
        P("group"),
        P("group", None),
        P("group", None),
        P("group", None),
        P(("replica", "group"), None),
    )
    return jax.shard_map(
        per_device,
        mesh=mesh,
        in_specs=placed,
        out_specs=(
            P(("replica", "group"), None),
            P(("replica", "group"), None),
            P("group"),
            P("group", None),
            P("group", None),
            P("group", None),
            P("group", None),
            P("group"),
            P("group", None),
            P("group", None),
            P("group", None),
        ),
        check_vma=False,
    )
```
